512 devices in a mesh: row: 32 (over y_hi, z), col: 16 (over y_lo, x, core).
Axes of the slice: x: 4, y: 4 (y_hi: 2, y_lo: 2; y = y_hi * 2 + y_lo), z: 16, core: 2. Of those that a mesh axis runs over, the one named last changes fastest.
Arguments:
- pair_norm: bfloat16 [512, 512, 128], P('row', 'col'), may hold values from -6 to 6
- out_hat: bfloat16 [512, 512, 128], P('row', 'col'), may hold values from -4 to 4
- out_rstd: float32 [512, 512], P('row', 'col'), may hold values from 0.02 to 0.2
- grad_out: bfloat16 [512, 512, 128], P('row', 'col'), may hold values from -6 to 6
- token_mask: int32 [512], replicated, may hold values 0 or 1
- w_in: bfloat16 [128, 512], replicated, may hold values from -0.5 to 0.5
- w_gate: bfloat16 [128, 128], replicated, may hold values from -0.5 to 0.5
- w_out: bfloat16 [128, 128], replicated, may hold values from -0.5 to 0.5
- ln_gain: float32 [128], replicated, may hold values from 0.1 to 1.9
Outputs:
- d_pair: bfloat16 [512, 512, 128], P('row', 'col')
- d_win: float32 [128, 512], replicated
- d_wgate: float32 [128, 128], replicated
- d_wout: float32 [128, 128], replicated
- d_gain: float32 [128], replicated
The draws below stay inside these ranges and needn't reach their ends.
All inputs are finite; a program needn't handle non-finite values.
Results may differ from the reference program's by a relative error of at most 0.0073.
Values may be sent and summed in bfloat16 or wider, within the bound.
A program may use at most 64 MiB of HBM per device.

```python
import math
import jax
import jax.numpy as jnp
from jax import lax

C = 128
N = 512


def plant(values, own_key, smallest, high):
    extent = values.shape
    place = [jax.random.randint(jax.random.fold_in(own_key, axis), (), 0, extent[axis]) for axis in range(len(extent))]
    values = values.at[tuple(place)].set(smallest)
    longest = extent.index(max(extent))
    place[longest] = (place[longest] + 1) % extent[longest]
    return values.at[tuple(place)].set(high)


def steps_of(rng, extent, cuts, least, top_value):
    factor_of = 1.0
    for position, parts in cuts:
        draws = jax.random.uniform(jax.random.fold_in(jax.random.fold_in(rng, 6), position), (parts,), jnp.float32, least / len(cuts), top_value / len(cuts))
        factor_of = factor_of * jnp.repeat(jnp.exp(draws), extent[position] // parts).reshape((-1,) + (1,) * (len(extent) - 1 - position))
    return factor_of


def scatter_about(rng, extent, scale, limit, split=(), dtype=jnp.bfloat16):
    drawn = scale * jax.random.normal(rng, extent, jnp.float32)
    if split:
        drawn = drawn * steps_of(rng, extent, split, -0.22, 0.18)
    return jnp.clip(drawn, -limit, limit).astype(dtype)


def setup_inputs(seed: int = 0) -> dict:
    key_of = jax.random.split(jax.random.key(seed), 10)
    return {
        "pair_norm": scatter_about(key_of[0], (N, N, C), 1.0, 6.0, ((0, 32), (1, 16))),
        "out_hat": scatter_about(key_of[1], (N, N, C), 1.0, 4.0, ((0, 32), (1, 16))),
        "out_rstd": jnp.clip(jnp.exp(math.log(0.2) - 2.3025851 * jax.random.uniform(key_of[2], (N, N), jnp.float32) ** steps_of(key_of[2], (N, N), ((0, 32), (1, 16)), -0.2, 0.2)), 0.02, 0.2),
        "grad_out": scatter_about(key_of[3], (N, N, C), 1.0, 6.0, ((0, 32), (1, 16))),
        "token_mask": plant((jax.random.randint(key_of[4], (N,), 0, 8) < 7).astype(jnp.int32), jax.random.fold_in(key_of[4], 1), 0, 1),
        "w_in": scatter_about(key_of[5], (C, 4 * C), C ** -0.5, 0.5),
        "w_gate": scatter_about(key_of[6], (C, C), C ** -0.5, 0.5),
        "w_out": scatter_about(key_of[7], (C, C), C ** -0.5, 0.5),
        "ln_gain": jnp.clip(1.0 + 0.18 * jax.random.normal(key_of[8], (C,), jnp.float32), 0.1, 1.9),
    }


def one_channel(operands):
    left_c, right_c, mix_c = operands
    grad_left = jnp.dot(right_c, mix_c.T, preferred_element_type=jnp.float32)
    grad_right = jnp.dot(left_c, mix_c, preferred_element_type=jnp.float32)
    return grad_left.astype(jnp.bfloat16), grad_right.astype(jnp.bfloat16)


def reference(pair_norm, out_hat, out_rstd, grad_out, token_mask, w_in, w_gate, w_out, ln_gain):
    token_count = token_mask.shape[0]
    width = pair_norm.shape[2]
    mask_float = token_mask.astype(jnp.float32)
    pair_mask = (mask_float[:, None] * mask_float[None, :])[:, :, None]
    flat_pair = pair_norm.reshape(-1, width)
    projected = jnp.dot(flat_pair, w_in, preferred_element_type=jnp.float32).reshape(token_count, token_count, 4 * width)
    value_a = projected[..., :width]
    logit_a = projected[..., width:2 * width]
    value_b = projected[..., 2 * width:3 * width]
    logit_b = projected[..., 3 * width:]
    sigma_a = jax.nn.sigmoid(logit_a)
    sigma_b = jax.nn.sigmoid(logit_b)
    left = (pair_mask * sigma_a * value_a).astype(jnp.bfloat16)
    right = (pair_mask * sigma_b * value_b).astype(jnp.bfloat16)
    gate = jax.nn.sigmoid(jnp.dot(flat_pair, w_gate, preferred_element_type=jnp.float32))
    normed = out_hat.reshape(-1, width).astype(jnp.float32)
    scaled = (normed * ln_gain).astype(jnp.bfloat16)
    output = jnp.dot(scaled, w_out, preferred_element_type=jnp.float32)
    grad_flat = grad_out.reshape(-1, width).astype(jnp.float32)
    gated_grad = (grad_flat * gate).astype(jnp.bfloat16)
    gate_grad = (grad_flat * output * gate * (1.0 - gate)).astype(jnp.bfloat16)
    d_wout = jnp.dot(scaled.T, gated_grad, preferred_element_type=jnp.float32) / token_count
    d_wgate = jnp.dot(flat_pair.T, gate_grad, preferred_element_type=jnp.float32) / token_count
    grad_scaled = jnp.dot(gated_grad, w_out.T, preferred_element_type=jnp.float32)
    d_gain = jnp.sum(grad_scaled * normed, axis=0) / token_count
    grad_normed = grad_scaled * ln_gain
    grad_mix = out_rstd.reshape(-1, 1) * (grad_normed - jnp.mean(grad_normed, axis=-1, keepdims=True)
                                          - normed * jnp.mean(grad_normed * normed, axis=-1, keepdims=True))
    grad_mix = grad_mix.astype(jnp.bfloat16).reshape(token_count, token_count, width)
    left_cf, right_cf = lax.map(one_channel, (left.transpose(2, 0, 1), right.transpose(2, 0, 1), grad_mix.transpose(2, 0, 1)))
    grad_left = left_cf.transpose(1, 2, 0).astype(jnp.float32)
    grad_right = right_cf.transpose(1, 2, 0).astype(jnp.float32)
    grad_proj = jnp.concatenate([
        grad_left * pair_mask * sigma_a,
        grad_left * pair_mask * value_a * sigma_a * (1.0 - sigma_a),
        grad_right * pair_mask * sigma_b,
        grad_right * pair_mask * value_b * sigma_b * (1.0 - sigma_b)], axis=-1).astype(jnp.bfloat16).reshape(-1, 4 * width)
    d_win = jnp.dot(flat_pair.T, grad_proj, preferred_element_type=jnp.float32) / token_count
    d_pair = (jnp.dot(grad_proj, w_in.T, preferred_element_type=jnp.float32)
              + jnp.dot(gate_grad, w_gate.T, preferred_element_type=jnp.float32))
    d_pair = d_pair.astype(jnp.bfloat16).reshape(token_count, token_count, width)
    return d_pair, d_win, d_wgate, d_wout, d_gain
```

```python
import jax
import jax.numpy as jnp
from jax import lax
from jax.experimental import pallas as pl
from jax.experimental.pallas import tpu as pltpu
from jax.sharding import PartitionSpec as P

F32, BF16 = jnp.float32, jnp.bfloat16
MESH = pl.DeviceIdType.MESH

TOKENS = 512
WIDTH = 128
ROWS, COLS = 16, 32
PAIRS = ROWS * COLS
RING = 16
BANKS = 2
ACROSS = 16
PLANE = BANKS * ACROSS
SLOTS = WIDTH // PLANE
CHUNK = 128 // SLOTS


def mm(a, b, ca, cb):
    return lax.dot_general(a, b, (((ca,), (cb,)), ((), ())), preferred_element_type=F32)


def swap_chunks(parts):
    lane = lax.broadcasted_iota(jnp.int32, parts[0].shape, 1)
    low = lane < 64
    even = lax.rem(lane // CHUNK, 2) == 0
    a, b, c, d = parts
    a, c = jnp.where(low, a, pltpu.roll(c, 64, 1)), jnp.where(low, pltpu.roll(a, 64, 1), c)
    b, d = jnp.where(low, b, pltpu.roll(d, 64, 1)), jnp.where(low, pltpu.roll(b, 64, 1), d)
    a, b = jnp.where(even, a, pltpu.roll(b, 32, 1)), jnp.where(even, pltpu.roll(a, 96, 1), b)
    c, d = jnp.where(even, c, pltpu.roll(d, 32, 1)), jnp.where(even, pltpu.roll(c, 96, 1), d)
    return a, b, c, d


def to_tiles(values, work):
    parts = []
    for slot in range(SLOTS):
        block = values[slot * PLANE : (slot + 1) * PLANE]
        parts.append(jnp.concatenate([block[:, g * 128 : (g + 1) * 128] for g in range(4)], axis=0))
    for low, part in enumerate(swap_chunks(parts)):
        for g in range(4):
            work[pl.ds(4 * g + low, PLANE, stride=ROWS), :] = part[g * PLANE : (g + 1) * PLANE]
    return work[...].astype(BF16).reshape(PLANE, ROWS, 128)


def from_tiles(tiles, work):
    work[...] = tiles.astype(F32).reshape(PLANE * ROWS, 128)
    parts = []
    for low in range(4):
        parts.append(
            jnp.concatenate(
                [work[pl.ds(4 * g + low, PLANE, stride=ROWS), :] for g in range(4)], axis=0
            )
        )
    out = []
    for part in swap_chunks(parts):
        out.append(
            jnp.concatenate([part[g * PLANE : (g + 1) * PLANE] for g in range(4)], axis=1)
        )
    return jnp.concatenate(out, axis=0)


def gather_slab(tiles):
    tiles = tiles.astype(F32).reshape(BANKS, 4, 4, ROWS, 128)
    parts = [tiles[:, :, q].reshape(BANKS * 4 * ROWS, 128) for q in range(4)]
    out = []
    for part in swap_chunks(parts):
        part = part.reshape(BANKS, 4, ROWS, 128)
        out.append(
            jnp.concatenate([part[:, g].reshape(BANKS * ROWS, 128) for g in range(4)], axis=1)
        )
    return jnp.concatenate(out, axis=0)


def scatter_slab(slab):
    parts = []
    for slot in range(SLOTS):
        block = slab[slot * BANKS * ROWS : (slot + 1) * BANKS * ROWS]
        block = [
            block[:, g * 128 : (g + 1) * 128].reshape(BANKS, 1, ROWS, 128) for g in range(4)
        ]
        parts.append(jnp.concatenate(block, axis=1).reshape(BANKS * 4 * ROWS, 128))
    out = [
        part.reshape(BANKS, 4, 1, ROWS, 128) for part in swap_chunks(parts)
    ]
    return jnp.concatenate(out, axis=2).reshape(PLANE, ROWS, 128).astype(BF16)


def kernel(
    pair_ref, hat_ref, rstd_ref, grad_ref, mask_ref, win_ref, wgate_ref, wout_ref, gain_ref,
    dpair_ref, dwin_ref, dwgate_ref, dwout_ref, dgain_ref,
    work, mix_out, mix_in, lr_out, lr_in, back_out, back_in,
    held, right_diag, left_cols, left_sums, right_sums, factors, proj,
    small_out, small_in, small_sum, small_row, small_mine, small_part, small_all,
    win_out, win_in, win_sum, win_row, win_mine, win_part, win_all,
    ring_send, ring_recv, send_sems, recv_sems,
):
    row, col = lax.axis_index("row"), lax.axis_index("col")
    bank, z = row // RING, lax.rem(row, RING)
    me = bank * ACROSS + col

    def plane_id(peer):
        return ((peer // ACROSS) * RING + z, lax.rem(peer, ACROSS))

    def ring_id(place):
        return (bank * RING + place, col)

    barrier = pltpu.get_barrier_semaphore()

    @pl.loop(1, PLANE)
    def _(t):
        pl.semaphore_signal(
            barrier, inc=1, device_id=plane_id(lax.rem(me + t, PLANE)), device_id_type=MESH
        )

    @pl.loop(1, RING)
    def _(t):
        pl.semaphore_signal(
            barrier, inc=1, device_id=ring_id(lax.rem(z + t, RING)), device_id_type=MESH
        )

    def plane_send(source, target, k):
        @pl.loop(1, PLANE)
        def _(t):
            peer = lax.rem(me + t, PLANE)
            pltpu.make_async_remote_copy(
                src_ref=source(peer), dst_ref=target.at[me],
                send_sem=send_sems.at[k], recv_sem=recv_sems.at[k],
                device_id=plane_id(peer), device_id_type=MESH,
            ).start()

    def ring_send_rows(source, target, k):
        @pl.loop(1, RING)
        def _(t):
            peer = lax.rem(z + t, RING)
            pltpu.make_async_remote_copy(
                src_ref=source(peer), dst_ref=target.at[pl.ds(z, 1)],
                send_sem=send_sems.at[k], recv_sem=recv_sems.at[k],
                device_id=ring_id(peer), device_id_type=MESH,
            ).start()

    def wait_bytes(ref, sem):
        pltpu.make_async_copy(ref, ref, sem).wait()

    def wait_many(target, count, k):
        wait_bytes(target.at[pl.ds(0, count - 1)], recv_sems.at[k])

    def hop(way, s, part):
        step = 1 if way == 0 else RING - 1
        block = lax.rem(z + (RING - 1) * step * (s - 1), RING)
        return pltpu.make_async_remote_copy(
            src_ref=held.at[block, part], dst_ref=held.at[block, part],
            send_sem=ring_send.at[way, s - 1, part], recv_sem=ring_recv.at[way, s - 1, part],
            device_id=ring_id(lax.rem(z + step, RING)), device_id_type=MESH,
        )

    x = pair_ref[...].reshape(PAIRS, WIDTH)
    hat = hat_ref[...].reshape(PAIRS, WIDTH).astype(F32).T
    grad = grad_ref[...].reshape(PAIRS, WIDTH).astype(F32).T
    diagonal = lax.broadcasted_iota(jnp.int32, (WIDTH, WIDTH), 0) == lax.broadcasted_iota(
        jnp.int32, (WIDTH, WIDTH), 1
    )
    gain = jnp.sum(jnp.where(diagonal, gain_ref[...], 0.0), axis=1, keepdims=True)
    pair_mask = mask_ref[...]
    gate = jax.nn.sigmoid(mm(wgate_ref[...], x, 0, 1))
    gated = (grad * gate).astype(BF16)
    scaled_grad = mm(wout_ref[...], gated, 1, 0)
    h = scaled_grad * gain
    mean_h = jnp.mean(h, axis=0, keepdims=True)
    mean_hx = jnp.mean(h * hat, axis=0, keepdims=True)
    mix = rstd_ref[...] * (h - mean_h - hat * mean_hx)
    mix_out[...] = to_tiles(mix, work)
    mix_in[me] = mix_out[me]
    pl.semaphore_wait(barrier, PLANE + RING - 2)
    plane_send(lambda peer: mix_out.at[peer], mix_in, 0)

    projected = mm(win_ref[...], x, 0, 1)
    value_a, logit_a = projected[:WIDTH], projected[WIDTH : 2 * WIDTH]
    value_b, logit_b = projected[2 * WIDTH : 3 * WIDTH], projected[3 * WIDTH :]
    sigma_a, sigma_b = jax.nn.sigmoid(logit_a), jax.nn.sigmoid(logit_b)
    masked_a, masked_b = pair_mask * sigma_a, pair_mask * sigma_b
    lr_out[:, :ROWS] = to_tiles(masked_a * value_a, work)
    lr_out[:, ROWS:] = to_tiles(masked_b * value_b, work)
    lr_in[me] = lr_out[me]
    plane_send(lambda peer: lr_out.at[peer], lr_in, 1)
    factors[0] = masked_a
    factors[1] = masked_a * value_a * (1.0 - sigma_a)
    factors[2] = masked_b
    factors[3] = masked_b * value_b * (1.0 - sigma_b)

    wait_many(mix_in, PLANE, 0)
    slab = gather_slab(mix_in[...]).astype(BF16)
    for slot in range(SLOTS):
        held[z, slot // 2, :, (slot % 2) * TOKENS : (slot % 2 + 1) * TOKENS] = slab[
            slot * BANKS * ROWS : (slot + 1) * BANKS * ROWS
        ]
    for part in range(2):
        for way in range(2):
            hop(way, 1, part).start()

    scaled = (hat * gain).astype(BF16)
    output = mm(wout_ref[...], scaled, 0, 0)
    gate_grad = (grad * output * gate * (1.0 - gate)).astype(BF16)
    proj[4 * WIDTH :] = gate_grad
    small_out[: PLANE // 2, :8] = mm(x, gate_grad, 0, 1).reshape(PLANE // 2, 8, WIDTH)
    small_out[PLANE // 2 :, :8] = mm(scaled, gated, 1, 1).reshape(PLANE // 2, 8, WIDTH)
    part_gain = jnp.sum(scaled_grad * hat, axis=1, keepdims=True)
    part_gain = jnp.sum(jnp.where(diagonal, part_gain, 0.0), axis=0, keepdims=True)
    small_out[:, 8:] = jnp.broadcast_to(part_gain[None], (PLANE, 8, WIDTH))
    small_in[me] = small_out[me]
    plane_send(lambda peer: small_out.at[peer], small_in, 2)

    wait_many(lr_in, PLANE, 1)
    left_cols[...] = gather_slab(lr_in[:, :ROWS]).T.astype(BF16)
    right = gather_slab(lr_in[:, ROWS:]).astype(BF16)
    right_diag[...] = jnp.zeros_like(right_diag)
    for slot in range(SLOTS):
        rows = slice(slot * BANKS * ROWS, (slot + 1) * BANKS * ROWS)
        right_diag[slot // 2, rows, (slot % 2) * TOKENS : (slot % 2 + 1) * TOKENS] = right[rows]
    right_sums[...] = jnp.zeros_like(right_sums)

    def contract(part, blocks):
        mixes = jnp.concatenate([held[block, part] for block in blocks], axis=0)
        places = [
            pl.ds(pl.multiple_of(b * (TOKENS // BANKS) + block * ROWS, ROWS), ROWS)
            for block in blocks
            for b in range(BANKS)
        ]
        sums = mm(mixes, right_diag[part], 1, 1)
        for n, place in enumerate(places):
            piece = sums[n * ROWS : (n + 1) * ROWS]
            if part:
                piece = piece + left_sums[place]
            left_sums[place] = piece
        lefts = jnp.concatenate([left_cols[place] for place in places], axis=0)
        for c in range(2):
            rows = slice((2 * part + c) * BANKS * ROWS, (2 * part + c + 1) * BANKS * ROWS)
            right_sums[rows] += mm(
                lefts[:, rows], mixes[:, c * TOKENS : (c + 1) * TOKENS], 0, 0
            )

    contract(0, [z])
    contract(1, [z])

    def ring_step(s, last):
        for part in range(2):
            for way in range(2):
                hop(way, s, part).wait_recv()
                if not last or way == part:
                    hop(way, s + 1, part).start()
            contract(part, [lax.rem(z + RING - s, RING), lax.rem(z + s, RING)])

    def close(total, row_in, mine, part, full, k):
        row_in[pl.ds(z, 1)] = total[pl.ds(z, 1)]
        ring_send_rows(lambda peer: total.at[pl.ds(peer, 1)], row_in, k)

    ring_step(1, False)
    ring_step(2, False)
    wait_many(small_in, PLANE, 2)
    small_sum[...] = jnp.sum(small_in[...], axis=0)
    small_row[pl.ds(z, 1)] = small_sum[pl.ds(z, 1)]
    ring_send_rows(lambda peer: small_sum.at[pl.ds(peer, 1)], small_row, 3)
    ring_step(3, False)
    ring_step(4, False)
    wait_many(small_row, RING, 3)
    small_mine[...] = jnp.sum(small_row[...], axis=0, keepdims=True) * (1.0 / TOKENS)
    small_part[pl.ds(z, 1)] = small_mine[...]
    ring_send_rows(lambda peer: small_mine, small_part, 4)
    ring_step(5, False)
    ring_step(6, False)
    wait_many(small_part, RING, 4)
    small_all[me] = small_part[:8]
    plane_send(lambda peer: small_part.at[pl.ds(0, 8)], small_all, 5)
    ring_step(7, True)
    for part in range(2):
        hop(part, RING // 2, part).wait_recv()
        contract(part, [lax.rem(z + RING // 2, RING)])

    back_out[:, :ROWS] = scatter_slab(left_sums[...].T)
    back_out[:, ROWS:] = scatter_slab(right_sums[...])
    back_in[me] = back_out[me]
    plane_send(lambda peer: back_out.at[peer], back_in, 6)
    wait_many(small_all, PLANE, 5)
    dwgate_ref[...] = small_all[: PLANE // 2].reshape(WIDTH, WIDTH)
    dwout_ref[...] = small_all[PLANE // 2 :].reshape(WIDTH, WIDTH)
    dgain_ref[...] = small_part[8:9]

    wait_many(back_in, PLANE, 6)
    grad_left = from_tiles(back_in[:, :ROWS], work)
    proj[:WIDTH] = (grad_left * factors[0]).astype(BF16)
    proj[WIDTH : 2 * WIDTH] = (grad_left * factors[1]).astype(BF16)
    grad_right = from_tiles(back_in[:, ROWS:], work)
    proj[2 * WIDTH : 3 * WIDTH] = (grad_right * factors[2]).astype(BF16)
    proj[3 * WIDTH : 4 * WIDTH] = (grad_right * factors[3]).astype(BF16)

    win_out[...] = mm(proj[: 4 * WIDTH], x, 1, 0).reshape(PLANE, ROWS, WIDTH)
    win_in[me] = win_out[me]
    plane_send(lambda peer: win_out.at[peer], win_in, 7)
    weights = jnp.concatenate([win_ref[...], wgate_ref[...]], axis=1)
    d_pair = mm(weights, proj[...], 1, 0)
    dpair_ref[...] = d_pair.T.astype(BF16).reshape(ROWS, COLS, WIDTH)
    wait_many(win_in, PLANE, 7)
    win_sum[...] = jnp.sum(win_in[...], axis=0)
    win_row[pl.ds(z, 1)] = win_sum[pl.ds(z, 1)]
    ring_send_rows(lambda peer: win_sum.at[pl.ds(peer, 1)], win_row, 8)
    wait_many(win_row, RING, 8)
    win_mine[...] = jnp.sum(win_row[...], axis=0, keepdims=True) * (1.0 / TOKENS)
    win_part[pl.ds(z, 1)] = win_mine[...]
    ring_send_rows(lambda peer: win_mine, win_part, 9)
    wait_many(win_part, RING, 9)
    win_all[me] = win_part[...]
    plane_send(lambda peer: win_part, win_all, 10)
    wait_many(win_all, PLANE, 10)
    dwin_ref[...] = win_all[...].reshape(4 * WIDTH, WIDTH).T

    for k, ref in enumerate(
        [mix_in, lr_in, small_in, None, None, small_all, back_in, win_in, None, None, win_all]
    ):
        if ref is None:
            wait_bytes(win_row.at[pl.ds(0, RING - 1)], send_sems.at[k])
        else:
            wait_bytes(ref.at[pl.ds(0, PLANE - 1)], send_sems.at[k])
    for s in range(1, RING // 2 + 1):
        for part in range(2):
            for way in range(2):
                if s < RING // 2 or way == part:
                    hop(way, s, part).wait_send()


def shards(pair_norm, out_hat, out_rstd, grad_out, token_mask, w_in, w_gate, w_out, ln_gain):
    row, col = lax.axis_index("row"), lax.axis_index("col")
    mask = token_mask.astype(F32)
    mask_rows = lax.dynamic_slice_in_dim(mask, row * ROWS, ROWS)
    mask_cols = lax.dynamic_slice_in_dim(mask, col * COLS, COLS)
    pair_mask = (mask_rows[:, None] * mask_cols[None, :]).reshape(1, PAIRS)
    tile = (ROWS, COLS, WIDTH)
    vmem = pl.BlockSpec(memory_space=pltpu.VMEM)
    reduction = lambda rows: [
        pltpu.VMEM((PLANE, ROWS, WIDTH), F32),
        pltpu.VMEM((PLANE, ROWS, WIDTH), F32),
        pltpu.VMEM((RING, WIDTH), F32),
        pltpu.VMEM((RING, WIDTH), F32),
        pltpu.VMEM((1, WIDTH), F32),
        pltpu.VMEM((RING, WIDTH), F32),
        pltpu.VMEM((PLANE, rows, WIDTH), F32),
    ]
    d_pair, d_win, d_wgate, d_wout, d_gain = pl.pallas_call(
        kernel,
        out_shape=(
            jax.ShapeDtypeStruct(tile, BF16),
            jax.ShapeDtypeStruct((WIDTH, 4 * WIDTH), F32),
            jax.ShapeDtypeStruct((WIDTH, WIDTH), F32),
            jax.ShapeDtypeStruct((WIDTH, WIDTH), F32),
            jax.ShapeDtypeStruct((1, WIDTH), F32),
        ),
        in_specs=[vmem] * 9,
        out_specs=[vmem] * 5,
        scratch_shapes=[
            pltpu.VMEM((PAIRS, WIDTH), F32),
            pltpu.VMEM((PLANE, ROWS, WIDTH), BF16),
            pltpu.VMEM((PLANE, ROWS, WIDTH), BF16),
            pltpu.VMEM((PLANE, 2 * ROWS, WIDTH), BF16),
            pltpu.VMEM((PLANE, 2 * ROWS, WIDTH), BF16),
            pltpu.VMEM((PLANE, 2 * ROWS, WIDTH), BF16),
            pltpu.VMEM((PLANE, 2 * ROWS, WIDTH), BF16),
            pltpu.VMEM((RING, 2, BANKS * ROWS, 2 * TOKENS), BF16),
            pltpu.VMEM((2, WIDTH, 2 * TOKENS), BF16),
            pltpu.VMEM((TOKENS, WIDTH), BF16),
            pltpu.VMEM((TOKENS, WIDTH), F32),
            pltpu.VMEM((WIDTH, TOKENS), F32),
            pltpu.VMEM((4, WIDTH, PAIRS), F32),
            pltpu.VMEM((5 * WIDTH, PAIRS), BF16),
            *reduction(8),
            *reduction(ROWS),
            pltpu.SemaphoreType.DMA((2, RING // 2, 2)),
            pltpu.SemaphoreType.DMA((2, RING // 2, 2)),
            pltpu.SemaphoreType.DMA((11,)),
            pltpu.SemaphoreType.DMA((11,)),
        ],
        compiler_params=pltpu.CompilerParams(
            collective_id=0, has_side_effects=True, vmem_limit_bytes=40 * 1024 * 1024
        ),
    )(
        pair_norm, out_hat, out_rstd.reshape(1, PAIRS), grad_out, pair_mask,
        w_in, w_gate, w_out, ln_gain.reshape(1, WIDTH),
    )
    return d_pair, d_win, d_wgate, d_wout, d_gain.reshape(WIDTH)


def solution(mesh):
    tile = P("row", "col", None)
    in_specs = (tile, tile, P("row", "col"), tile, P(), P(), P(), P(), P())
    out_specs = (tile, P(), P(), P(), P())
    return jax.shard_map(shards, mesh=mesh, in_specs=in_specs, out_specs=out_specs, check_vma=False)
```

```python
import jax
import jax.numpy as jnp
from jax import lax
from jax.experimental import pallas as pl
from jax.experimental.pallas import tpu as pltpu
from jax.sharding import PartitionSpec as P

F32, BF16 = jnp.float32, jnp.bfloat16
MESH = pl.DeviceIdType.MESH

TOKENS = 512
WIDTH = 128
ROWS, COLS = 16, 32
PAIRS = ROWS * COLS
RING = 16
BANKS = 2
ACROSS = 16
PLANE = BANKS * ACROSS
SLOTS = WIDTH // PLANE
CHUNK = 128 // SLOTS


def mm(a, b, ca, cb):
    return lax.dot_general(a, b, (((ca,), (cb,)), ((), ())), preferred_element_type=F32)


def swap_chunks(parts):
    lane = lax.broadcasted_iota(jnp.int32, parts[0].shape, 1)
    low = lane < 64
    even = lax.rem(lane // CHUNK, 2) == 0
    a, b, c, d = parts
    a, c = jnp.where(low, a, pltpu.roll(c, 64, 1)), jnp.where(low, pltpu.roll(a, 64, 1), c)
    b, d = jnp.where(low, b, pltpu.roll(d, 64, 1)), jnp.where(low, pltpu.roll(b, 64, 1), d)
    a, b = jnp.where(even, a, pltpu.roll(b, 32, 1)), jnp.where(even, pltpu.roll(a, 96, 1), b)
    c, d = jnp.where(even, c, pltpu.roll(d, 32, 1)), jnp.where(even, pltpu.roll(c, 96, 1), d)
    return a, b, c, d


def to_tiles(values, work):
    parts = []
    for slot in range(SLOTS):
        block = values[slot * PLANE : (slot + 1) * PLANE]
        parts.append(jnp.concatenate([block[:, g * 128 : (g + 1) * 128] for g in range(4)], axis=0))
    for low, part in enumerate(swap_chunks(parts)):
        for g in range(4):
            work[pl.ds(4 * g + low, PLANE, stride=ROWS), :] = part[g * PLANE : (g + 1) * PLANE]
    return work[...].astype(BF16).reshape(PLANE, ROWS, 128)


def from_tiles(tiles, work):
    work[...] = tiles.astype(F32).reshape(PLANE * ROWS, 128)
    parts = []
    for low in range(4):
        parts.append(
            jnp.concatenate(
                [work[pl.ds(4 * g + low, PLANE, stride=ROWS), :] for g in range(4)], axis=0
            )
        )
    out = []
    for part in swap_chunks(parts):
        out.append(
            jnp.concatenate([part[g * PLANE : (g + 1) * PLANE] for g in range(4)], axis=1)
        )
    return jnp.concatenate(out, axis=0)


def gather_slab(tiles):
    tiles = tiles.astype(F32).reshape(BANKS, 4, 4, ROWS, 128)
    parts = [tiles[:, :, q].reshape(BANKS * 4 * ROWS, 128) for q in range(4)]
    out = []
    for part in swap_chunks(parts):
        part = part.reshape(BANKS, 4, ROWS, 128)
        out.append(
            jnp.concatenate([part[:, g].reshape(BANKS * ROWS, 128) for g in range(4)], axis=1)
        )
    return jnp.concatenate(out, axis=0)


def scatter_slab(slab):
    parts = []
    for slot in range(SLOTS):
        block = slab[slot * BANKS * ROWS : (slot + 1) * BANKS * ROWS]
        block = [
            block[:, g * 128 : (g + 1) * 128].reshape(BANKS, 1, ROWS, 128) for g in range(4)
        ]
        parts.append(jnp.concatenate(block, axis=1).reshape(BANKS * 4 * ROWS, 128))
    out = [
        part.reshape(BANKS, 4, 1, ROWS, 128) for part in swap_chunks(parts)
    ]
    return jnp.concatenate(out, axis=2).reshape(PLANE, ROWS, 128).astype(BF16)


def kernel(
    pair_hbm, hat_hbm, rstd_hbm, grad_hbm, mask_hbm, win_hbm, wgate_hbm, wout_hbm, gain_hbm,
    dpair_hbm, dwin_hbm, dsmall_hbm, dgain_hbm,
    pair_ref, hat_ref, rstd_ref, grad_ref, mask_ref, win_ref, wgate_ref, wout_ref, gain_ref,
    dpair_ref, dwin_ref, dsmall_ref, dgain_ref, work, mix_out, mix_in, lr_out, lr_in, factor_out, factor_in, back_out, back_in,
    held, right_diag, left_cols, left_sums, right_sums, factors, slab_factors, slab_proj, proj,
    pairs_all, small_out, small_in, small_half, small_ring, small_mine, small_all,
    win_half, win_ring, win_mine, win_all,
    load_sems, save_sems, ring_send, ring_recv, send_sems, recv_sems, x_send, x_recv,
):
    row, col = lax.axis_index("row"), lax.axis_index("col")
    bank, z = row // RING, lax.rem(row, RING)
    me = bank * ACROSS + col
    core = lax.rem(col, 2)
    at_x, at_y = lax.rem(col // 2, 4), bank * 2 + col // 8

    def plane_id(peer):
        return ((peer // ACROSS) * RING + z, lax.rem(peer, ACROSS))

    def ring_id(place):
        return (bank * RING + place, col)

    barrier = pltpu.get_barrier_semaphore()

    @pl.loop(1, PLANE)
    def _(t):
        pl.semaphore_signal(
            barrier, inc=1, device_id=plane_id(lax.rem(me + t, PLANE)), device_id_type=MESH
        )

    for t in (1, RING - 1):
        pl.semaphore_signal(
            barrier, inc=1, device_id=ring_id(lax.rem(z + t, RING)), device_id_type=MESH
        )

    loads = [
        pltpu.make_async_copy(source, target, load_sems.at[k])
        for k, (source, target) in enumerate(
            [
                (pair_hbm, pair_ref), (wgate_hbm, wgate_ref), (grad_hbm, grad_ref),
                (wout_hbm, wout_ref), (hat_hbm, hat_ref), (gain_hbm, gain_ref),
                (rstd_hbm, rstd_ref), (win_hbm, win_ref), (mask_hbm, mask_ref),
            ]
        )
    ]
    for load in loads:
        load.start()

    saves = [
        pltpu.make_async_copy(source, target, save_sems.at[k])
        for k, (source, target) in enumerate(
            [
                (dpair_ref, dpair_hbm), (dwin_ref, dwin_hbm),
                (dsmall_ref, dsmall_hbm), (dgain_ref, dgain_hbm),
            ]
        )
    ]
    received, sent = [], []

    def plane_send(source, target, k):
        received.append((target, PLANE, k))
        sent.append((target, PLANE, k))

        @pl.loop(1, PLANE)
        def _(t):
            peer = lax.rem(me + t, PLANE)
            pltpu.make_async_remote_copy(
                src_ref=source(peer), dst_ref=target.at[me],
                send_sem=send_sems.at[k], recv_sem=recv_sems.at[k],
                device_id=plane_id(peer), device_id_type=MESH,
            ).start()

    def ring_copy(source, target, offset, k):
        return pltpu.make_async_remote_copy(
            src_ref=source, dst_ref=target.at[z],
            send_sem=send_sems.at[k], recv_sem=recv_sems.at[k],
            device_id=ring_id(lax.rem(z + offset, RING)), device_id_type=MESH,
        )

    def ring_share(source, target, k, farthest=True):
        received.append((target, RING, k))
        sent.append((target, RING, k))

        @pl.loop(1, RING - 1)
        def _(t):
            ring_copy(source, target, t + t // (RING // 2), k).start()

        if farthest:
            ring_copy(source, target, RING // 2, k).start()

    def wait_bytes(ref, sem):
        pltpu.make_async_copy(ref, ref, sem).wait()

    def wait_many(target, count, k):
        received.remove((target, count, k))
        wait_bytes(target.at[pl.ds(0, count - 1)], recv_sems.at[k])

    hops, arrivals = [], []

    def drain():
        for target, count, k in received:
            wait_bytes(target.at[pl.ds(0, count - 1)], recv_sems.at[k])
        for target, count, k in sent:
            wait_bytes(target.at[pl.ds(0, count - 1)], send_sems.at[k])
        for key in arrivals:
            hop(*key).wait_recv()
        for key in hops:
            hop(*key).wait_send()
        for key in incoming:
            piece(*key).wait_recv()
        for key in outgoing:
            piece(*key).wait_send()

    def start_hop(way, s, part):
        hops.append((way, s, part))
        arrivals.append((way, s, part))
        hop(way, s, part).start()

    def await_hop(way, s, part):
        arrivals.remove((way, s, part))
        hop(way, s, part).wait_recv()

    def hop(way, s, part):
        step = 1 if way == 0 else RING - 1
        block = lax.rem(z + (RING - 1) * step * (s - 1), RING)
        return pltpu.make_async_remote_copy(
            src_ref=held.at[block, part], dst_ref=held.at[block, part],
            send_sem=ring_send.at[way, s - 1, part], recv_sem=ring_recv.at[way, s - 1, part],
            device_id=ring_id(lax.rem(z + step, RING)), device_id_type=MESH,
        )

    outgoing, incoming = [], []

    def piece(kind, dy, dx):
        ty, tx = lax.rem(at_y + dy, 4), lax.rem(at_x + dx, 4)
        rows = pl.ds(0, ROWS)
        to_y, to_x, to_core = at_y, at_x, core
        if kind == "core":
            to_core, k = 1 - core, 24 + 4 * dy + dx
        if kind[0] == "y":
            way = 1 if kind[1] == "+" else 3
            to_y = lax.rem(at_y + way, 4)
            if dy:
                rows = pl.ds(0 if way == 1 else ROWS // 2, ROWS // 2)
            k = (0 if way == 1 else 1) + (2 if dy else 0)
        if kind[0] == "x":
            way = 1 if kind[1] == "+" else 3
            to_x = lax.rem(at_x + way, 4)
            if dx:
                rows = pl.ds(0 if way == 1 else ROWS // 2, ROWS // 2)
            k = 4 + dy * 4 + (0 if way == 1 else 1) + (2 if dx else 0)
        place = pairs_all.at[ty // 2, rows, lax.rem(ty, 2) * 8 + tx * 2 + core]
        return pltpu.make_async_remote_copy(
            src_ref=place, dst_ref=place, send_sem=x_send.at[k], recv_sem=x_recv.at[k],
            device_id=((to_y // 2) * RING + z, lax.rem(to_y, 2) * 8 + to_x * 2 + to_core),
            device_id_type=MESH,
        )

    def pass_on(kind, dy, dx):
        outgoing.append((kind, dy, dx))
        incoming.append((kind, dy, dx))
        piece(kind, dy, dx).start()

    def take(kind, dy, dx):
        incoming.remove((kind, dy, dx))
        piece(kind, dy, dx).wait_recv()

    def relay(stage):
        if stage == 0:
            pairs_all[bank, :, col] = pair_ref[...]
            for way in "+-":
                pass_on("y" + way, 0, 0)
                pass_on("x" + way, 0, 0)
            pass_on("core", 0, 0)
        if stage == 1:
            take("y+", 0, 0)
            pass_on("y+", 3, 0)
            take("y-", 0, 0)
            pass_on("y-", 1, 0)
            for dy in (3, 1):
                for way in "+-":
                    pass_on("x" + way, dy, 0)
                pass_on("core", dy, 0)
            take("x+", 0, 0)
            pass_on("x+", 0, 3)
            take("x-", 0, 0)
            pass_on("x-", 0, 1)
            pass_on("core", 0, 3)
            pass_on("core", 0, 1)
        if stage == 2:
            take("y+", 3, 0)
            take("y-", 1, 0)
            for way in "+-":
                pass_on("x" + way, 2, 0)
            pass_on("core", 2, 0)
            for dy in (3, 1):
                take("x+", dy, 0)
                pass_on("x+", dy, 3)
                take("x-", dy, 0)
                pass_on("x-", dy, 1)
                pass_on("core", dy, 3)
                pass_on("core", dy, 1)
            take("x+", 0, 3)
            take("x-", 0, 1)
            pass_on("core", 0, 2)
        if stage == 3:
            take("x+", 2, 0)
            pass_on("x+", 2, 3)
            take("x-", 2, 0)
            pass_on("x-", 2, 1)
            pass_on("core", 2, 3)
            pass_on("core", 2, 1)
            for dy in (3, 1):
                take("x+", dy, 3)
                take("x-", dy, 1)
                pass_on("core", dy, 2)
        if stage == 4:
            take("x+", 2, 3)
            take("x-", 2, 1)
            pass_on("core", 2, 2)
        if stage == 5:
            for dy in range(4):
                for dx in range(4):
                    take("core", dy, dx)

    def column(values):
        return jnp.sum(jnp.where(diagonal, values, 0.0), axis=1, keepdims=True)

    diagonal = lax.broadcasted_iota(jnp.int32, (WIDTH, WIDTH), 0) == lax.broadcasted_iota(
        jnp.int32, (WIDTH, WIDTH), 1
    )
    for load in loads[:3]:
        load.wait()
    x = pair_ref[...].reshape(PAIRS, WIDTH)
    gate = jax.nn.sigmoid(mm(wgate_ref[...], x, 0, 1))
    grad = grad_ref[...].reshape(PAIRS, WIDTH).astype(F32).T
    gated = (grad * gate).astype(BF16)
    for load in loads[3:7]:
        load.wait()
    scaled_grad = mm(wout_ref[...], gated, 1, 0)
    hat = hat_ref[...].reshape(PAIRS, WIDTH).astype(F32).T
    gain = column(gain_ref[...])
    spread = jnp.concatenate([rstd_ref[...]] * ROWS, axis=1)
    own_row = lax.broadcasted_iota(jnp.int32, spread.shape, 1) // COLS
    own_row = own_row == lax.broadcasted_iota(jnp.int32, spread.shape, 0)
    rstd = jnp.sum(jnp.where(own_row, spread, 0.0), axis=0, keepdims=True)
    h = scaled_grad * gain
    mean_h = jnp.mean(h, axis=0, keepdims=True)
    mean_hx = jnp.mean(h * hat, axis=0, keepdims=True)
    mix = rstd * (h - mean_h - hat * mean_hx)
    mix_out[...] = to_tiles(mix, work)
    mix_in[me] = mix_out[me]
    for load in loads[7:]:
        load.wait()
    pl.semaphore_wait(barrier, PLANE + 1)
    plane_send(lambda peer: mix_out.at[peer], mix_in, 0)

    token = lax.broadcasted_iota(jnp.int32, (TOKENS, PAIRS), 0)
    pair = lax.broadcasted_iota(jnp.int32, (TOKENS, PAIRS), 1)
    mask = jnp.broadcast_to(mask_ref[...].astype(F32), (8, TOKENS)).astype(BF16)
    mask_row = mm(mask, (token == row * ROWS + pair // COLS).astype(BF16), 1, 0)
    mask_col = mm(mask, (token == col * COLS + lax.rem(pair, COLS)).astype(BF16), 1, 0)
    pair_mask = (mask_row * mask_col)[:1]
    projected = mm(win_ref[...], x, 0, 1)
    value_a, logit_a = projected[:WIDTH], projected[WIDTH : 2 * WIDTH]
    value_b, logit_b = projected[2 * WIDTH : 3 * WIDTH], projected[3 * WIDTH :]
    sigma_a, sigma_b = jax.nn.sigmoid(logit_a), jax.nn.sigmoid(logit_b)
    masked_a, masked_b = pair_mask * sigma_a, pair_mask * sigma_b
    lr_out[:, :ROWS] = to_tiles(masked_a * value_a, work)
    lr_out[:, ROWS:] = to_tiles(masked_b * value_b, work)
    lr_in[me] = lr_out[me]
    plane_send(lambda peer: lr_out.at[peer], lr_in, 1)
    factors[0] = masked_a
    factors[1] = masked_a * value_a * (1.0 - sigma_a)
    factors[2] = masked_b
    factors[3] = masked_b * value_b * (1.0 - sigma_b)

    wait_many(mix_in, PLANE, 0)
    slab = gather_slab(mix_in[...]).astype(BF16)
    for slot in range(SLOTS):
        held[z, slot // 2, :, (slot % 2) * TOKENS : (slot % 2 + 1) * TOKENS] = slab[
            slot * BANKS * ROWS : (slot + 1) * BANKS * ROWS
        ]
    for part in range(2):
        for way in range(2):
            start_hop(way, 1, part)
    relay(0)

    wait_many(lr_in, PLANE, 1)
    left_cols[...] = gather_slab(lr_in[:, :ROWS]).T.astype(BF16)
    right = gather_slab(lr_in[:, ROWS:]).astype(BF16)
    right_diag[...] = jnp.zeros_like(right_diag)
    for slot in range(SLOTS):
        rows = slice(slot * BANKS * ROWS, (slot + 1) * BANKS * ROWS)
        right_diag[slot // 2, rows, (slot % 2) * TOKENS : (slot % 2 + 1) * TOKENS] = right[rows]
    right_sums[...] = jnp.zeros_like(right_sums)

    def contract(part, blocks):
        mixes = jnp.concatenate([held[block, part] for block in blocks], axis=0)
        places = [
            pl.ds(pl.multiple_of(b * (TOKENS // BANKS) + block * ROWS, ROWS), ROWS)
            for block in blocks
            for b in range(BANKS)
        ]
        sums = mm(mixes, right_diag[part], 1, 1)
        for n, place in enumerate(places):
            values = sums[n * ROWS : (n + 1) * ROWS]
            if part:
                values = values + left_sums[place]
            left_sums[place] = values
        lefts = jnp.concatenate([left_cols[place] for place in places], axis=0)
        for c in range(2):
            rows = slice((2 * part + c) * BANKS * ROWS, (2 * part + c + 1) * BANKS * ROWS)
            right_sums[rows] += mm(
                lefts[:, rows], mixes[:, c * TOKENS : (c + 1) * TOKENS], 0, 0
            )

    def ring_step(s, last):
        for part in range(2):
            for way in range(2):
                await_hop(way, s, part)
                if not last or way == part:
                    start_hop(way, s + 1, part)
            contract(part, [lax.rem(z + RING - s, RING), lax.rem(z + s, RING)])

    contract(0, [z])
    contract(1, [z])
    ring_step(1, False)

    for n in range(4):
        factor_out[:, n * ROWS : (n + 1) * ROWS] = to_tiles(factors[n], work)
    factor_in[me] = factor_out[me]
    plane_send(lambda peer: factor_out.at[peer], factor_in, 2)
    ring_step(2, False)

    scaled = (hat * gain).astype(BF16)
    output = mm(wout_ref[...], scaled, 0, 0)
    gate_grad = (grad * output * gate * (1.0 - gate)).astype(BF16)
    proj[4 * WIDTH :] = gate_grad
    small_out[: PLANE // 2, :8] = mm(x, gate_grad, 0, 1).reshape(PLANE // 2, 8, WIDTH)
    small_out[PLANE // 2 :, :8] = mm(scaled, gated, 1, 1).reshape(PLANE // 2, 8, WIDTH)
    part_gain = jnp.sum(scaled_grad * hat, axis=1, keepdims=True)
    part_gain = jnp.sum(jnp.where(diagonal, part_gain, 0.0), axis=0, keepdims=True)
    small_out[:, 8:] = jnp.broadcast_to(part_gain[None], (PLANE, 8, WIDTH))
    small_in[me] = small_out[me]
    plane_send(lambda peer: small_out.at[peer], small_in, 3)
    ring_step(3, False)
    relay(1)
    ring_step(4, False)

    wait_many(factor_in, PLANE, 2)
    for n in range(4):
        slab_factors[n] = gather_slab(factor_in[:, n * ROWS : (n + 1) * ROWS]).astype(BF16)
    ring_step(5, False)
    relay(2)
    wait_many(small_in, PLANE, 3)
    small_half[...] = jnp.sum(small_in[...], axis=0).astype(BF16)
    small_ring[z] = small_half[...]
    ring_step(6, False)
    relay(3)
    ring_step(7, True)
    ring_share(small_half, small_ring, 4, False)
    relay(4)
    for part in range(2):
        await_hop(part, RING // 2, part)
        contract(part, [lax.rem(z + RING // 2, RING)])
    ring_copy(small_half, small_ring, RING // 2, 4).start()

    left_grad = left_sums[...].T
    for n in range(2):
        values = left_grad if n == 0 else right_sums[...]
        values = values.astype(BF16).astype(F32)
        for m in range(2):
            terms = values * slab_factors[2 * n + m].astype(F32)
            for g in range(4):
                slab_proj[g, (2 * n + m) * WIDTH : (2 * n + m + 1) * WIDTH] = terms[
                    :, g * 128 : (g + 1) * 128
                ]
    relay(5)
    total = jnp.zeros((4 * SLOTS, WIDTH), F32)
    for k in range(BANKS * ROWS):
        terms = jnp.concatenate(
            [slab_proj[g, pl.ds(k, 4 * SLOTS, stride=BANKS * ROWS), :] for g in range(4)], axis=1
        )
        pairs = pairs_all[k // ROWS, k % ROWS].reshape(TOKENS, WIDTH)
        total = total + mm(terms.astype(BF16), pairs, 1, 0)
    win_half[...] = total.astype(BF16)
    win_ring[z] = win_half[...]
    ring_share(win_half, win_ring, 5)

    back_out[:, :ROWS] = scatter_slab(left_grad)
    back_out[:, ROWS:] = scatter_slab(right_sums[...])
    back_in[me] = back_out[me]
    plane_send(lambda peer: back_out.at[peer], back_in, 6)

    def ring_total(ring):
        return jnp.sum(ring[...].astype(F32), axis=0) * (1.0 / TOKENS)

    wait_many(small_ring, RING, 4)
    small_mine[...] = ring_total(small_ring)
    dgain_ref[...] = small_mine[8:9]
    saves[3].start()
    small_all[me] = small_mine[:8]
    plane_send(lambda peer: small_mine.at[pl.ds(0, 8)], small_all, 7)

    wait_many(win_ring, RING, 5)
    win_mine[...] = ring_total(win_ring)
    win_all[me] = win_mine[...]
    plane_send(lambda peer: win_mine, win_all, 8)

    wait_many(back_in, PLANE, 6)
    grad_left = from_tiles(back_in[:, :ROWS], work)
    proj[:WIDTH] = (grad_left * factors[0]).astype(BF16)
    proj[WIDTH : 2 * WIDTH] = (grad_left * factors[1]).astype(BF16)
    grad_right = from_tiles(back_in[:, ROWS:], work)
    proj[2 * WIDTH : 3 * WIDTH] = (grad_right * factors[2]).astype(BF16)
    proj[3 * WIDTH : 4 * WIDTH] = (grad_right * factors[3]).astype(BF16)
    weights = jnp.concatenate([win_ref[...], wgate_ref[...]], axis=1)
    d_pair = mm(weights, proj[...], 1, 0)
    dpair_ref[...] = d_pair.T.astype(BF16).reshape(ROWS, COLS, WIDTH)
    saves[0].start()

    wait_many(small_all, PLANE, 7)
    dsmall_ref[...] = small_all[...].reshape(2 * WIDTH, WIDTH)
    saves[2].start()
    wait_many(win_all, PLANE, 8)
    work[...] = win_all[...].reshape(4 * WIDTH, WIDTH)
    dwin_ref[...] = jnp.concatenate(
        [work[pl.ds(n, PLANE, stride=4 * SLOTS), :] for n in range(4 * SLOTS)], axis=0
    ).T
    saves[1].start()
    drain()
    for save in saves:
        save.wait()


def finish(dpair, dwin, dsmall, dgain, dpair_out, dwin_out, dwgate_out, dwout_out, dgain_out, *rest):
    held, loads, saves = rest[:4], rest[4], rest[5]
    sources = [dpair, dwin, dsmall, dgain]
    first = [
        pltpu.make_async_copy(source, target, loads.at[k])
        for k, (source, target) in enumerate(zip(sources, held))
    ]
    last = [
        pltpu.make_async_copy(source, target, saves.at[k])
        for k, (source, target) in enumerate(
            [
                (held[0], dpair_out),
                (held[1], dwin_out),
                (held[2].at[pl.ds(0, WIDTH)], dwgate_out),
                (held[2].at[pl.ds(WIDTH, WIDTH)], dwout_out),
                (held[3], dgain_out),
            ]
        )
    ]
    for copy in first:
        copy.start()
    for k, copies in enumerate([last[:1], last[1:2], last[2:4], last[4:]]):
        first[k].wait()
        for copy in copies:
            copy.start()
    for copy in last:
        copy.wait()


def shards(pair_norm, out_hat, out_rstd, grad_out, token_mask, w_in, w_gate, w_out, ln_gain):
    tile = (ROWS, COLS, WIDTH)
    square = (WIDTH, WIDTH)
    hbm = pl.BlockSpec(memory_space=pltpu.HBM)
    shape = jax.ShapeDtypeStruct
    tiles = lambda rows, dtype: pltpu.VMEM((PLANE, rows, WIDTH), dtype)
    results = pl.pallas_call(
        kernel,
        out_shape=(
            shape(tile, BF16),
            shape((WIDTH, 4 * WIDTH), F32),
            shape((2 * WIDTH, WIDTH), F32),
            shape((1, WIDTH), F32),
        ),
        in_specs=[hbm] * 9,
        out_specs=[hbm] * 4,
        scratch_shapes=[
            pltpu.VMEM(tile, BF16),
            pltpu.VMEM(tile, BF16),
            pltpu.VMEM((ROWS, COLS), F32),
            pltpu.VMEM(tile, BF16),
            pltpu.VMEM((1, TOKENS), jnp.int32),
            pltpu.VMEM((WIDTH, 4 * WIDTH), BF16),
            pltpu.VMEM(square, BF16),
            pltpu.VMEM(square, BF16),
            pltpu.VMEM((1, WIDTH), F32),
            pltpu.VMEM(tile, BF16),
            pltpu.VMEM((WIDTH, 4 * WIDTH), F32),
            pltpu.VMEM((2 * WIDTH, WIDTH), F32),
            pltpu.VMEM((1, WIDTH), F32),
            pltpu.VMEM((PAIRS, WIDTH), F32),
            *[tiles(ROWS, BF16)] * 2,
            *[tiles(2 * ROWS, BF16)] * 2,
            *[tiles(4 * ROWS, BF16)] * 2,
            *[tiles(2 * ROWS, BF16)] * 2,
            pltpu.VMEM((RING, 2, BANKS * ROWS, 2 * TOKENS), BF16),
            pltpu.VMEM((2, WIDTH, 2 * TOKENS), BF16),
            pltpu.VMEM((TOKENS, WIDTH), BF16),
            pltpu.VMEM((TOKENS, WIDTH), F32),
            pltpu.VMEM((WIDTH, TOKENS), F32),
            pltpu.VMEM((4, WIDTH, PAIRS), F32),
            pltpu.VMEM((4, WIDTH, TOKENS), BF16),
            pltpu.VMEM((4, 4 * WIDTH, 128), F32),
            pltpu.VMEM((5 * WIDTH, PAIRS), BF16),
            pltpu.VMEM((BANKS, ROWS, ACROSS, COLS, WIDTH), BF16),
            tiles(ROWS, F32),
            tiles(ROWS, F32),
            pltpu.VMEM((ROWS, WIDTH), BF16),
            pltpu.VMEM((RING, ROWS, WIDTH), BF16),
            pltpu.VMEM((ROWS, WIDTH), F32),
            tiles(8, F32),
            pltpu.VMEM((ROWS, WIDTH), BF16),
            pltpu.VMEM((RING, ROWS, WIDTH), BF16),
            pltpu.VMEM((ROWS, WIDTH), F32),
            tiles(ROWS, F32),
            pltpu.SemaphoreType.DMA((9,)),
            pltpu.SemaphoreType.DMA((4,)),
            pltpu.SemaphoreType.DMA((2, RING // 2, 2)),
            pltpu.SemaphoreType.DMA((2, RING // 2, 2)),
            pltpu.SemaphoreType.DMA((9,)),
            pltpu.SemaphoreType.DMA((9,)),
            pltpu.SemaphoreType.DMA((40,)),
            pltpu.SemaphoreType.DMA((40,)),
        ],
        compiler_params=pltpu.CompilerParams(
            collective_id=0, has_side_effects=True, vmem_limit_bytes=62 * 1024 * 1024
        ),
    )(
        pair_norm, out_hat, out_rstd, grad_out, token_mask.reshape(1, TOKENS),
        w_in, w_gate, w_out, ln_gain.reshape(1, WIDTH),
    )
    d_pair, d_win, d_wgate, d_wout, d_gain = pl.pallas_call(
        finish,
        out_shape=(
            shape(tile, BF16),
            shape((WIDTH, 4 * WIDTH), F32),
            shape(square, F32),
            shape(square, F32),
            shape((1, WIDTH), F32),
        ),
        in_specs=[hbm] * 4,
        out_specs=[hbm] * 5,
        scratch_shapes=[
            pltpu.VMEM(tile, BF16),
            pltpu.VMEM((WIDTH, 4 * WIDTH), F32),
            pltpu.VMEM((2 * WIDTH, WIDTH), F32),
            pltpu.VMEM((1, WIDTH), F32),
            pltpu.SemaphoreType.DMA((4,)),
            pltpu.SemaphoreType.DMA((5,)),
        ],
        compiler_params=pltpu.CompilerParams(vmem_limit_bytes=62 * 1024 * 1024),
    )(*results)
    return d_pair, d_win, d_wgate, d_wout, d_gain.reshape(WIDTH)


def solution(mesh):
    tile = P("row", "col", None)
    in_specs = (tile, tile, P("row", "col"), tile, P(), P(), P(), P(), P())
    out_specs = (tile, P(), P(), P(), P())
    return jax.shard_map(shards, mesh=mesh, in_specs=in_specs, out_specs=out_specs, check_vma=False)
```

```python
import jax
import jax.numpy as jnp
from jax import lax
from jax.experimental import pallas as pl
from jax.experimental.pallas import tpu as pltpu
from jax.sharding import PartitionSpec as P

F32, BF16 = jnp.float32, jnp.bfloat16
MESH = pl.DeviceIdType.MESH

TOKENS = 512
WIDTH = 128
ROWS, COLS = 16, 32
PAIRS = ROWS * COLS
RING = 16
BANKS = 2
ACROSS = 16
PLANE = BANKS * ACROSS
SLOTS = WIDTH // PLANE
CHUNK = 128 // SLOTS
FAR_FIRST = (2, 3, 1, 0)


def mm(a, b, ca, cb):
    return lax.dot_general(a, b, (((ca,), (cb,)), ((), ())), preferred_element_type=F32)


def swap_chunks(parts):
    lane = lax.broadcasted_iota(jnp.int32, parts[0].shape, 1)
    low = lane < 64
    even = lax.rem(lane // CHUNK, 2) == 0
    a, b, c, d = parts
    a, c = jnp.where(low, a, pltpu.roll(c, 64, 1)), jnp.where(low, pltpu.roll(a, 64, 1), c)
    b, d = jnp.where(low, b, pltpu.roll(d, 64, 1)), jnp.where(low, pltpu.roll(b, 64, 1), d)
    a, b = jnp.where(even, a, pltpu.roll(b, 32, 1)), jnp.where(even, pltpu.roll(a, 96, 1), b)
    c, d = jnp.where(even, c, pltpu.roll(d, 32, 1)), jnp.where(even, pltpu.roll(c, 96, 1), d)
    return a, b, c, d


def to_tiles(values, work):
    parts = []
    for slot in range(SLOTS):
        block = values[slot * PLANE : (slot + 1) * PLANE]
        parts.append(jnp.concatenate([block[:, g * 128 : (g + 1) * 128] for g in range(4)], axis=0))
    for low, part in enumerate(swap_chunks(parts)):
        for g in range(4):
            work[pl.ds(4 * g + low, PLANE, stride=ROWS), :] = part[g * PLANE : (g + 1) * PLANE]
    return work[...].astype(BF16).reshape(PLANE, ROWS, 128)


def from_tiles(tiles, work):
    work[...] = tiles.astype(F32).reshape(PLANE * ROWS, 128)
    parts = []
    for low in range(4):
        parts.append(
            jnp.concatenate(
                [work[pl.ds(4 * g + low, PLANE, stride=ROWS), :] for g in range(4)], axis=0
            )
        )
    out = []
    for part in swap_chunks(parts):
        out.append(
            jnp.concatenate([part[g * PLANE : (g + 1) * PLANE] for g in range(4)], axis=1)
        )
    return jnp.concatenate(out, axis=0)


def gather_slab(tiles):
    tiles = tiles.astype(F32).reshape(BANKS, 4, 4, ROWS, 128)
    parts = [tiles[:, :, q].reshape(BANKS * 4 * ROWS, 128) for q in range(4)]
    out = []
    for part in swap_chunks(parts):
        part = part.reshape(BANKS, 4, ROWS, 128)
        out.append(
            jnp.concatenate([part[:, g].reshape(BANKS * ROWS, 128) for g in range(4)], axis=1)
        )
    return jnp.concatenate(out, axis=0)


def scatter_slab(slab):
    parts = []
    for slot in range(SLOTS):
        block = slab[slot * BANKS * ROWS : (slot + 1) * BANKS * ROWS]
        block = [
            block[:, g * 128 : (g + 1) * 128].reshape(BANKS, 1, ROWS, 128) for g in range(4)
        ]
        parts.append(jnp.concatenate(block, axis=1).reshape(BANKS * 4 * ROWS, 128))
    out = [
        part.reshape(BANKS, 4, 1, ROWS, 128) for part in swap_chunks(parts)
    ]
    return jnp.concatenate(out, axis=2).reshape(PLANE, ROWS, 128).astype(BF16)


def kernel(
    pair_hbm, hat_hbm, rstd_hbm, grad_hbm, mask_hbm, win_hbm, wgate_hbm, wout_hbm, gain_hbm,
    dpair_hbm, dwin_hbm, dsmall_hbm, dgain_hbm,
    pair_ref, hat_ref, rstd_ref, grad_ref, mask_ref, win_ref, wgate_ref, wout_ref, gain_ref,
    dpair_ref, dwin_ref, dsmall_ref, dgain_ref, work, mix_out, mix_in, lr_out, lr_in, factor_out, factor_in, back_out, back_in,
    held, right_diag, left_cols, left_sums, right_sums, factors, slab_factors, slab_proj, proj,
    pairs_all, small_out, small_in, small_half, small_ring, small_mine, small_all,
    win_half, win_ring, win_mine, win_all,
    load_sems, save_sems, ring_send, ring_recv, send_sems, recv_sems, x_send, x_recv,
):
    row, col = lax.axis_index("row"), lax.axis_index("col")
    bank, z = row // RING, lax.rem(row, RING)
    me = bank * ACROSS + col
    core = lax.rem(col, 2)
    at_x, at_y = lax.rem(col // 2, 4), bank * 2 + col // 8

    def plane_id(peer):
        return ((peer // ACROSS) * RING + z, lax.rem(peer, ACROSS))

    def ring_id(place):
        return (bank * RING + place, col)

    def far_first(t):
        across, along, other = t // 8, lax.rem(t // 2, 4), 1 - lax.rem(t, 2)
        dy, dx = (3 - n + (2 * n - 1) * (1 - n // 2) for n in (across, along))
        return (
            lax.rem(at_y + dy, 4) * 8
            + lax.rem(at_x + dx, 4) * 2
            + lax.rem(core + other, 2)
        )

    plane_y = [lax.rem(at_y + n, 4) for n in range(4)]
    plane_row = [(y // 2) * RING + z for y in plane_y]
    plane_col = [lax.rem(y, 2) * 8 for y in plane_y]
    plane_x = [
        [lax.rem(at_x + n, 4) * 2 + lax.rem(core + other, 2) for other in range(2)]
        for n in range(4)
    ]

    barrier = pltpu.get_barrier_semaphore()

    @pl.loop(0, PLANE - 1)
    def _(t):
        pl.semaphore_signal(
            barrier, inc=1, device_id=plane_id(far_first(t)), device_id_type=MESH
        )

    for t in (1, RING - 1):
        pl.semaphore_signal(
            barrier, inc=1, device_id=ring_id(lax.rem(z + t, RING)), device_id_type=MESH
        )

    loads = [
        pltpu.make_async_copy(source, target, load_sems.at[k])
        for k, (source, target) in enumerate(
            [
                (pair_hbm, pair_ref), (wgate_hbm, wgate_ref), (grad_hbm, grad_ref),
                (wout_hbm, wout_ref), (hat_hbm, hat_ref), (gain_hbm, gain_ref),
                (rstd_hbm, rstd_ref), (win_hbm, win_ref), (mask_hbm, mask_ref),
            ]
        )
    ]
    for load in loads:
        load.start()

    saves = [
        pltpu.make_async_copy(source, target, save_sems.at[k])
        for k, (source, target) in enumerate(
            [
                (dpair_ref, dpair_hbm), (dwin_ref, dwin_hbm),
                (dsmall_ref, dsmall_hbm), (dgain_ref, dgain_hbm),
            ]
        )
    ]
    received, sent = [], []

    def plane_send(source, target, k):
        received.append((target, PLANE, k))
        sent.append((target, PLANE, k))

        for across, along in ((a, b) for a in FAR_FIRST for b in FAR_FIRST):
            for other in (1, 0):
                if across or along or other:
                    peer = plane_y[across] * 8 + plane_x[along][other]
                    pltpu.make_async_remote_copy(
                        src_ref=source(peer), dst_ref=target.at[me],
                        send_sem=send_sems.at[k], recv_sem=recv_sems.at[k],
                        device_id=(plane_row[across], plane_col[across] + plane_x[along][other]),
                        device_id_type=MESH,
                    ).start()

    def ring_copy(source, target, offset, k):
        return pltpu.make_async_remote_copy(
            src_ref=source, dst_ref=target.at[z],
            send_sem=send_sems.at[k], recv_sem=recv_sems.at[k],
            device_id=ring_id(lax.rem(z + offset, RING)), device_id_type=MESH,
        )

    def ring_share(source, target, k, farthest=True):
        received.append((target, RING, k))
        sent.append((target, RING, k))

        @pl.loop(0 if farthest else 1, RING - 1)
        def _(t):
            offset = RING // 2 + ((t + 1) // 2) * (2 * lax.rem(t + 1, 2) - 1)
            ring_copy(source, target, offset, k).start()

    def wait_bytes(ref, sem):
        pltpu.make_async_copy(ref, ref, sem).wait()

    def wait_many(target, count, k):
        received.remove((target, count, k))
        wait_bytes(target.at[pl.ds(0, count - 1)], recv_sems.at[k])

    hops, arrivals = [], []

    def drain():
        for target, count, k in received:
            wait_bytes(target.at[pl.ds(0, count - 1)], recv_sems.at[k])
        for target, count, k in sent:
            wait_bytes(target.at[pl.ds(0, count - 1)], send_sems.at[k])
        for key in arrivals:
            hop(*key).wait_recv()
        for key in hops:
            hop(*key).wait_send()
        for key in incoming:
            piece(*key).wait_recv()
        for key in outgoing:
            piece(*key).wait_send()

    def start_hop(way, s, slot):
        hops.append((way, s, slot))
        arrivals.append((way, s, slot))
        hop(way, s, slot).start()

    def await_hop(way, s, slot):
        arrivals.remove((way, s, slot))
        hop(way, s, slot).wait_recv()

    def hop(way, s, slot):
        step = 1 if way == 0 else RING - 1
        block = lax.rem(z + (RING - 1) * step * (s - 1), RING)
        return pltpu.make_async_remote_copy(
            src_ref=held.at[block, slot], dst_ref=held.at[block, slot],
            send_sem=ring_send.at[way, s - 1, slot], recv_sem=ring_recv.at[way, s - 1, slot],
            device_id=ring_id(lax.rem(z + step, RING)), device_id_type=MESH,
        )

    outgoing, incoming = [], []

    def piece(kind, dy, dx):
        ty, tx = lax.rem(at_y + dy, 4), lax.rem(at_x + dx, 4)
        rows = pl.ds(0, ROWS)
        to_y, to_x, to_core = at_y, at_x, core
        if kind == "core":
            to_core, k = 1 - core, 24 + 4 * dy + dx
        if kind[0] == "y":
            way = 1 if kind[1] == "+" else 3
            to_y = lax.rem(at_y + way, 4)
            if dy:
                rows = pl.ds(0 if way == 1 else ROWS // 2, ROWS // 2)
            k = (0 if way == 1 else 1) + (2 if dy else 0)
        if kind[0] == "x":
            way = 1 if kind[1] == "+" else 3
            to_x = lax.rem(at_x + way, 4)
            if dx:
                rows = pl.ds(0 if way == 1 else ROWS // 2, ROWS // 2)
            k = 4 + dy * 4 + (0 if way == 1 else 1) + (2 if dx else 0)
        place = pairs_all.at[ty // 2, rows, lax.rem(ty, 2) * 8 + tx * 2 + core]
        return pltpu.make_async_remote_copy(
            src_ref=place, dst_ref=place, send_sem=x_send.at[k], recv_sem=x_recv.at[k],
            device_id=((to_y // 2) * RING + z, lax.rem(to_y, 2) * 8 + to_x * 2 + to_core),
            device_id_type=MESH,
        )

    def pass_on(kind, dy, dx):
        outgoing.append((kind, dy, dx))
        incoming.append((kind, dy, dx))
        piece(kind, dy, dx).start()

    def take(kind, dy, dx):
        incoming.remove((kind, dy, dx))
        piece(kind, dy, dx).wait_recv()

    def relay(stage):
        if stage == 0:
            pairs_all[bank, :, col] = pair_ref[...]
            for way in "+-":
                pass_on("y" + way, 0, 0)
                pass_on("x" + way, 0, 0)
            pass_on("core", 0, 0)
        if stage == 1:
            take("y+", 0, 0)
            pass_on("y+", 3, 0)
            take("y-", 0, 0)
            pass_on("y-", 1, 0)
            for dy in (3, 1):
                for way in "+-":
                    pass_on("x" + way, dy, 0)
                pass_on("core", dy, 0)
            take("x+", 0, 0)
            pass_on("x+", 0, 3)
            take("x-", 0, 0)
            pass_on("x-", 0, 1)
            pass_on("core", 0, 3)
            pass_on("core", 0, 1)
        if stage == 2:
            take("y+", 3, 0)
            take("y-", 1, 0)
            for way in "+-":
                pass_on("x" + way, 2, 0)
            pass_on("core", 2, 0)
            for dy in (3, 1):
                take("x+", dy, 0)
                pass_on("x+", dy, 3)
                take("x-", dy, 0)
                pass_on("x-", dy, 1)
                pass_on("core", dy, 3)
                pass_on("core", dy, 1)
            take("x+", 0, 3)
            take("x-", 0, 1)
            pass_on("core", 0, 2)
        if stage == 3:
            take("x+", 2, 0)
            pass_on("x+", 2, 3)
            take("x-", 2, 0)
            pass_on("x-", 2, 1)
            pass_on("core", 2, 3)
            pass_on("core", 2, 1)
            for dy in (3, 1):
                take("x+", dy, 3)
                take("x-", dy, 1)
                pass_on("core", dy, 2)
        if stage == 4:
            take("x+", 2, 3)
            take("x-", 2, 1)
            pass_on("core", 2, 2)
        if stage == 5:
            for dy in range(4):
                for dx in range(4):
                    take("core", dy, dx)

    def column(values):
        return jnp.sum(jnp.where(diagonal, values, 0.0), axis=1, keepdims=True)

    diagonal = lax.broadcasted_iota(jnp.int32, (WIDTH, WIDTH), 0) == lax.broadcasted_iota(
        jnp.int32, (WIDTH, WIDTH), 1
    )
    for load in loads[:3]:
        load.wait()
    x = pair_ref[...].reshape(PAIRS, WIDTH)
    gate = jax.nn.sigmoid(mm(wgate_ref[...], x, 0, 1))
    grad = grad_ref[...].reshape(PAIRS, WIDTH).astype(F32).T
    gated = (grad * gate).astype(BF16)
    for load in loads[3:7]:
        load.wait()
    scaled_grad = mm(wout_ref[...], gated, 1, 0)
    hat = hat_ref[...].reshape(PAIRS, WIDTH).astype(F32).T
    gain = column(gain_ref[...])
    spread = jnp.concatenate([rstd_ref[...]] * ROWS, axis=1)
    own_row = lax.broadcasted_iota(jnp.int32, (1, PAIRS), 1) // COLS
    own_row = own_row == lax.broadcasted_iota(jnp.int32, spread.shape, 0)
    rstd = jnp.sum(jnp.where(own_row, spread, 0.0), axis=0, keepdims=True)
    h = scaled_grad * gain
    mean_h = jnp.mean(h, axis=0, keepdims=True)
    mean_hx = jnp.mean(h * hat, axis=0, keepdims=True)
    mix = rstd * (h - mean_h - hat * mean_hx)
    mix_out[...] = to_tiles(mix, work)
    mix_in[me] = mix_out[me]
    for load in loads[7:]:
        load.wait()
    pl.semaphore_wait(barrier, PLANE + 1)
    plane_send(lambda peer: mix_out.at[peer], mix_in, 0)

    token = lax.broadcasted_iota(jnp.int32, (TOKENS, PAIRS), 0)
    pair = lax.broadcasted_iota(jnp.int32, (1, PAIRS), 1)
    mask = jnp.broadcast_to(mask_ref[...].astype(F32), (8, TOKENS)).astype(BF16)
    one_hot = lambda place: jnp.where(token == place, 1.0, 0.0).astype(BF16)
    mask_row = mm(mask, one_hot(row * ROWS + pair // COLS), 1, 0)
    mask_col = mm(mask, one_hot(col * COLS + lax.rem(pair, COLS)), 1, 0)
    pair_mask = (mask_row * mask_col)[:1]
    projected = mm(win_ref[...], x, 0, 1)
    value_a, logit_a = projected[:WIDTH], projected[WIDTH : 2 * WIDTH]
    value_b, logit_b = projected[2 * WIDTH : 3 * WIDTH], projected[3 * WIDTH :]
    sigma_a, sigma_b = jax.nn.sigmoid(logit_a), jax.nn.sigmoid(logit_b)
    masked_a, masked_b = pair_mask * sigma_a, pair_mask * sigma_b
    lr_out[:, :ROWS] = to_tiles(masked_a * value_a, work)
    lr_out[:, ROWS:] = to_tiles(masked_b * value_b, work)
    lr_in[me] = lr_out[me]
    plane_send(lambda peer: lr_out.at[peer], lr_in, 1)
    factors[0] = masked_a
    factors[1] = masked_a * value_a * (1.0 - sigma_a)
    factors[2] = masked_b
    factors[3] = masked_b * value_b * (1.0 - sigma_b)

    wait_many(mix_in, PLANE, 0)
    slab = gather_slab(mix_in[...]).astype(BF16)
    for slot in range(SLOTS):
        held[z, slot] = slab[slot * BANKS * ROWS : (slot + 1) * BANKS * ROWS]
        for way in range(2):
            start_hop(way, 1, slot)


    wait_many(lr_in, PLANE, 1)
    left_cols[...] = gather_slab(lr_in[:, :ROWS]).T.astype(BF16)
    right = gather_slab(lr_in[:, ROWS:]).astype(BF16)
    right_diag[...] = jnp.zeros_like(right_diag)
    for slot in range(SLOTS):
        rows = slice(slot * BANKS * ROWS, (slot + 1) * BANKS * ROWS)
        right_diag[rows, slot * TOKENS : (slot + 1) * TOKENS] = right[rows]
    right_sums[...] = jnp.zeros_like(right_sums)

    def contract(blocks):
        mixes = [
            jnp.concatenate([held[block, slot] for block in blocks], axis=0)
            for slot in range(SLOTS)
        ]
        places = [
            pl.ds(pl.multiple_of(b * (TOKENS // BANKS) + block * ROWS, ROWS), ROWS)
            for block in blocks
            for b in range(BANKS)
        ]
        sums = mm(jnp.concatenate(mixes, axis=1), right_diag[...], 1, 1)
        for n, place in enumerate(places):
            left_sums[place] = sums[n * ROWS : (n + 1) * ROWS]
        lefts = jnp.concatenate([left_cols[place] for place in places], axis=0).astype(F32)
        lefts = lefts.T.astype(BF16)
        for slot in range(SLOTS):
            rows = slice(slot * BANKS * ROWS, (slot + 1) * BANKS * ROWS)
            right_sums[rows] += mm(lefts[rows], mixes[slot], 1, 0)

    def ring_step(s, last):
        for slot in range(SLOTS):
            for way in range(2):
                await_hop(way, s, slot)
                if not last or way == slot // 2:
                    start_hop(way, s + 1, slot)
        contract([lax.rem(z + RING - s, RING), lax.rem(z + s, RING)])

    contract([z])
    relay(0)
    ring_step(1, False)

    for n in range(4):
        factor_out[:, n * ROWS : (n + 1) * ROWS] = to_tiles(factors[n], work)
    factor_in[me] = factor_out[me]
    plane_send(lambda peer: factor_out.at[peer], factor_in, 2)
    ring_step(2, False)

    scaled = (hat * gain).astype(BF16)
    output = mm(wout_ref[...], scaled, 0, 0)
    gate_grad = (grad * output * gate * (1.0 - gate)).astype(BF16)
    proj[4 * WIDTH :] = gate_grad
    small_out[: PLANE // 2, :8] = mm(x, gate_grad, 0, 1).reshape(PLANE // 2, 8, WIDTH)
    small_out[PLANE // 2 :, :8] = mm(scaled, gated, 1, 1).reshape(PLANE // 2, 8, WIDTH)
    part_gain = jnp.sum(scaled_grad * hat, axis=1, keepdims=True)
    part_gain = jnp.sum(jnp.where(diagonal, part_gain, 0.0), axis=0, keepdims=True)
    small_out[:, 8:] = jnp.broadcast_to(part_gain[None], (PLANE, 8, WIDTH))
    small_in[me] = small_out[me]
    plane_send(lambda peer: small_out.at[peer], small_in, 3)
    ring_step(3, False)
    ring_step(4, False)
    relay(1)

    wait_many(factor_in, PLANE, 2)
    for n in range(4):
        slab_factors[n] = gather_slab(factor_in[:, n * ROWS : (n + 1) * ROWS]).astype(BF16)
    ring_step(5, False)
    wait_many(small_in, PLANE, 3)
    small_half[...] = jnp.sum(small_in[...], axis=0).astype(BF16)
    small_ring[z] = small_half[...]
    ring_step(6, False)
    relay(2)
    ring_step(7, True)
    ring_share(small_half, small_ring, 4, False)
    relay(3)
    for slot in range(SLOTS):
        await_hop(slot // 2, RING // 2, slot)
    ring_copy(small_half, small_ring, RING // 2, 4).start()
    relay(4)
    contract([lax.rem(z + RING // 2, RING)])

    left_grad = left_sums[...].T
    for n in range(2):
        values = left_grad if n == 0 else right_sums[...]
        values = values.astype(BF16).astype(F32)
        for m in range(2):
            terms = values * slab_factors[2 * n + m].astype(F32)
            for g in range(4):
                slab_proj[g, (2 * n + m) * WIDTH : (2 * n + m + 1) * WIDTH] = terms[
                    :, g * 128 : (g + 1) * 128
                ]
    relay(5)
    total = jnp.zeros((4 * SLOTS, WIDTH), F32)
    for k in range(BANKS * ROWS):
        terms = jnp.concatenate(
            [slab_proj[g, pl.ds(k, 4 * SLOTS, stride=BANKS * ROWS), :] for g in range(4)], axis=1
        )
        pairs = pairs_all[k // ROWS, k % ROWS].reshape(TOKENS, WIDTH)
        total = total + mm(terms.astype(BF16), pairs, 1, 0)
    win_half[...] = total.astype(BF16)
    win_ring[z] = win_half[...]
    ring_share(win_half, win_ring, 5)

    back_out[:, :ROWS] = scatter_slab(left_grad)
    back_out[:, ROWS:] = scatter_slab(right_sums[...])
    back_in[me] = back_out[me]
    plane_send(lambda peer: back_out.at[peer], back_in, 6)

    def ring_total(ring):
        return jnp.sum(ring[...].astype(F32), axis=0) * (1.0 / TOKENS)

    wait_many(small_ring, RING, 4)
    small_mine[...] = ring_total(small_ring)
    dgain_ref[...] = small_mine[8:9]
    saves[3].start()
    small_all[me] = small_mine[:8]
    plane_send(lambda peer: small_mine.at[pl.ds(0, 8)], small_all, 7)

    wait_many(win_ring, RING, 5)
    win_mine[...] = ring_total(win_ring).astype(BF16)
    win_all[me] = win_mine[...]
    plane_send(lambda peer: win_mine, win_all, 8)

    wait_many(back_in, PLANE, 6)
    grad_left = from_tiles(back_in[:, :ROWS], work)
    proj[:WIDTH] = (grad_left * factors[0]).astype(BF16)
    proj[WIDTH : 2 * WIDTH] = (grad_left * factors[1]).astype(BF16)
    grad_right = from_tiles(back_in[:, ROWS:], work)
    proj[2 * WIDTH : 3 * WIDTH] = (grad_right * factors[2]).astype(BF16)
    proj[3 * WIDTH : 4 * WIDTH] = (grad_right * factors[3]).astype(BF16)
    weights = jnp.concatenate([win_ref[...], wgate_ref[...]], axis=1)
    d_pair = mm(weights, proj[...], 1, 0)
    dpair_ref[...] = d_pair.T.astype(BF16).reshape(ROWS, COLS, WIDTH)
    saves[0].start()

    wait_many(small_all, PLANE, 7)
    dsmall_ref[...] = small_all[...].reshape(2 * WIDTH, WIDTH)
    saves[2].start()
    wait_many(win_all, PLANE, 8)
    work[...] = win_all[...].astype(F32).reshape(4 * WIDTH, WIDTH)
    dwin_ref[...] = jnp.concatenate(
        [work[pl.ds(n, PLANE, stride=4 * SLOTS), :] for n in range(4 * SLOTS)], axis=0
    ).T
    saves[1].start()
    drain()
    for save in saves:
        save.wait()


def finish(dpair, dwin, dsmall, dgain, dpair_out, dwin_out, dwgate_out, dwout_out, dgain_out, *rest):
    held, loads, saves = rest[:4], rest[4], rest[5]
    sources = [dpair, dwin, dsmall, dgain]
    first = [
        pltpu.make_async_copy(source, target, loads.at[k])
        for k, (source, target) in enumerate(zip(sources, held))
    ]
    last = [
        pltpu.make_async_copy(source, target, saves.at[k])
        for k, (source, target) in enumerate(
            [
                (held[0], dpair_out),
                (held[1], dwin_out),
                (held[2].at[pl.ds(0, WIDTH)], dwgate_out),
                (held[2].at[pl.ds(WIDTH, WIDTH)], dwout_out),
                (held[3], dgain_out),
            ]
        )
    ]
    for copy in first:
        copy.start()
    for k, copies in enumerate([last[:1], last[1:2], last[2:4], last[4:]]):
        first[k].wait()
        for copy in copies:
            copy.start()
    for copy in last:
        copy.wait()


def shards(pair_norm, out_hat, out_rstd, grad_out, token_mask, w_in, w_gate, w_out, ln_gain):
    tile = (ROWS, COLS, WIDTH)
    square = (WIDTH, WIDTH)
    hbm = pl.BlockSpec(memory_space=pltpu.HBM)
    shape = jax.ShapeDtypeStruct
    tiles = lambda rows, dtype: pltpu.VMEM((PLANE, rows, WIDTH), dtype)
    results = pl.pallas_call(
        kernel,
        out_shape=(
            shape(tile, BF16),
            shape((WIDTH, 4 * WIDTH), F32),
            shape((2 * WIDTH, WIDTH), F32),
            shape((1, WIDTH), F32),
        ),
        in_specs=[hbm] * 9,
        out_specs=[hbm] * 4,
        scratch_shapes=[
            pltpu.VMEM(tile, BF16),
            pltpu.VMEM(tile, BF16),
            pltpu.VMEM((ROWS, COLS), F32),
            pltpu.VMEM(tile, BF16),
            pltpu.VMEM((1, TOKENS), jnp.int32),
            pltpu.VMEM((WIDTH, 4 * WIDTH), BF16),
            pltpu.VMEM(square, BF16),
            pltpu.VMEM(square, BF16),
            pltpu.VMEM((1, WIDTH), F32),
            pltpu.VMEM(tile, BF16),
            pltpu.VMEM((WIDTH, 4 * WIDTH), F32),
            pltpu.VMEM((2 * WIDTH, WIDTH), F32),
            pltpu.VMEM((1, WIDTH), F32),
            pltpu.VMEM((PAIRS, WIDTH), F32),
            *[tiles(ROWS, BF16)] * 2,
            *[tiles(2 * ROWS, BF16)] * 2,
            *[tiles(4 * ROWS, BF16)] * 2,
            *[tiles(2 * ROWS, BF16)] * 2,
            pltpu.VMEM((RING, SLOTS, BANKS * ROWS, TOKENS), BF16),
            pltpu.VMEM((WIDTH, SLOTS * TOKENS), BF16),
            pltpu.VMEM((TOKENS, WIDTH), BF16),
            pltpu.VMEM((TOKENS, WIDTH), F32),
            pltpu.VMEM((WIDTH, TOKENS), F32),
            pltpu.VMEM((4, WIDTH, PAIRS), F32),
            pltpu.VMEM((4, WIDTH, TOKENS), BF16),
            pltpu.VMEM((4, 4 * WIDTH, 128), F32),
            pltpu.VMEM((5 * WIDTH, PAIRS), BF16),
            pltpu.VMEM((BANKS, ROWS, ACROSS, COLS, WIDTH), BF16),
            tiles(ROWS, F32),
            tiles(ROWS, F32),
            pltpu.VMEM((ROWS, WIDTH), BF16),
            pltpu.VMEM((RING, ROWS, WIDTH), BF16),
            pltpu.VMEM((ROWS, WIDTH), F32),
            tiles(8, F32),
            pltpu.VMEM((ROWS, WIDTH), BF16),
            pltpu.VMEM((RING, ROWS, WIDTH), BF16),
            pltpu.VMEM((ROWS, WIDTH), BF16),
            tiles(ROWS, BF16),
            pltpu.SemaphoreType.DMA((9,)),
            pltpu.SemaphoreType.DMA((4,)),
            pltpu.SemaphoreType.DMA((2, RING // 2, SLOTS)),
            pltpu.SemaphoreType.DMA((2, RING // 2, SLOTS)),
            pltpu.SemaphoreType.DMA((9,)),
            pltpu.SemaphoreType.DMA((9,)),
            pltpu.SemaphoreType.DMA((40,)),
            pltpu.SemaphoreType.DMA((40,)),
        ],
        compiler_params=pltpu.CompilerParams(
            collective_id=0, has_side_effects=True, vmem_limit_bytes=62 * 1024 * 1024
        ),
    )(
        pair_norm, out_hat, out_rstd, grad_out, token_mask.reshape(1, TOKENS),
        w_in, w_gate, w_out, ln_gain.reshape(1, WIDTH),
    )
    d_pair, d_win, d_wgate, d_wout, d_gain = pl.pallas_call(
        finish,
        out_shape=(
            shape(tile, BF16),
            shape((WIDTH, 4 * WIDTH), F32),
            shape(square, F32),
            shape(square, F32),
            shape((1, WIDTH), F32),
        ),
        in_specs=[hbm] * 4,
        out_specs=[hbm] * 5,
        scratch_shapes=[
            pltpu.VMEM(tile, BF16),
            pltpu.VMEM((WIDTH, 4 * WIDTH), F32),
            pltpu.VMEM((2 * WIDTH, WIDTH), F32),
            pltpu.VMEM((1, WIDTH), F32),
            pltpu.SemaphoreType.DMA((4,)),
            pltpu.SemaphoreType.DMA((5,)),
        ],
        compiler_params=pltpu.CompilerParams(vmem_limit_bytes=62 * 1024 * 1024),
    )(*results)
    return d_pair, d_win, d_wgate, d_wout, d_gain.reshape(WIDTH)


def solution(mesh):
    tile = P("row", "col", None)
    in_specs = (tile, tile, P("row", "col"), tile, P(), P(), P(), P(), P())
    out_specs = (tile, P(), P(), P(), P())
    return jax.shard_map(shards, mesh=mesh, in_specs=in_specs, out_specs=out_specs, check_vma=False)
```

```python
import jax
import jax.numpy as jnp
from jax import lax
from jax.experimental import pallas as pl
from jax.experimental.pallas import tpu as pltpu
from jax.sharding import PartitionSpec as P

F32, BF16 = jnp.float32, jnp.bfloat16
MESH = pl.DeviceIdType.MESH

TOKENS = 512
WIDTH = 128
ROWS, COLS = 16, 32
PAIRS = ROWS * COLS
RING = 16
BANKS = 2
ACROSS = 16
PLANE = BANKS * ACROSS
SLOTS = WIDTH // PLANE
CHUNK = 128 // SLOTS
FAR_FIRST = (2, 3, 1, 0)


def mm(a, b, ca, cb):
    return lax.dot_general(a, b, (((ca,), (cb,)), ((), ())), preferred_element_type=F32)


def swap_chunks(parts):
    lane = lax.broadcasted_iota(jnp.int32, parts[0].shape, 1)
    low = lane < 64
    even = lax.rem(lane // CHUNK, 2) == 0
    a, b, c, d = parts
    a, c = jnp.where(low, a, pltpu.roll(c, 64, 1)), jnp.where(low, pltpu.roll(a, 64, 1), c)
    b, d = jnp.where(low, b, pltpu.roll(d, 64, 1)), jnp.where(low, pltpu.roll(b, 64, 1), d)
    a, b = jnp.where(even, a, pltpu.roll(b, 32, 1)), jnp.where(even, pltpu.roll(a, 96, 1), b)
    c, d = jnp.where(even, c, pltpu.roll(d, 32, 1)), jnp.where(even, pltpu.roll(c, 96, 1), d)
    return a, b, c, d


def to_tiles(values, work):
    parts = []
    for slot in range(SLOTS):
        block = values[slot * PLANE : (slot + 1) * PLANE]
        parts.append(jnp.concatenate([block[:, g * 128 : (g + 1) * 128] for g in range(4)], axis=0))
    for low, part in enumerate(swap_chunks(parts)):
        for g in range(4):
            work[pl.ds(4 * g + low, PLANE, stride=ROWS), :] = part[g * PLANE : (g + 1) * PLANE]
    return work[...].astype(BF16).reshape(PLANE, ROWS, 128)


def from_tiles(tiles, work):
    work[...] = tiles.astype(F32).reshape(PLANE * ROWS, 128)
    parts = []
    for low in range(4):
        parts.append(
            jnp.concatenate(
                [work[pl.ds(4 * g + low, PLANE, stride=ROWS), :] for g in range(4)], axis=0
            )
        )
    out = []
    for part in swap_chunks(parts):
        out.append(
            jnp.concatenate([part[g * PLANE : (g + 1) * PLANE] for g in range(4)], axis=1)
        )
    return jnp.concatenate(out, axis=0)


def gather_slab(tiles):
    tiles = tiles.astype(F32).reshape(BANKS, 4, 4, ROWS, 128)
    parts = [tiles[:, :, q].reshape(BANKS * 4 * ROWS, 128) for q in range(4)]
    out = []
    for part in swap_chunks(parts):
        part = part.reshape(BANKS, 4, ROWS, 128)
        out.append(
            jnp.concatenate([part[:, g].reshape(BANKS * ROWS, 128) for g in range(4)], axis=1)
        )
    return jnp.concatenate(out, axis=0)


def scatter_slab(slab):
    parts = []
    for slot in range(SLOTS):
        block = slab[slot * BANKS * ROWS : (slot + 1) * BANKS * ROWS]
        block = [
            block[:, g * 128 : (g + 1) * 128].reshape(BANKS, 1, ROWS, 128) for g in range(4)
        ]
        parts.append(jnp.concatenate(block, axis=1).reshape(BANKS * 4 * ROWS, 128))
    out = [
        part.reshape(BANKS, 4, 1, ROWS, 128) for part in swap_chunks(parts)
    ]
    return jnp.concatenate(out, axis=2).reshape(PLANE, ROWS, 128).astype(BF16)


def kernel(
    pair_hbm, hat_hbm, rstd_hbm, grad_hbm, mask_hbm, win_hbm, wgate_hbm, wout_hbm, gain_hbm,
    dpair_hbm, dwin_hbm, dsmall_hbm, dgain_hbm,
    pair_ref, hat_ref, rstd_ref, grad_ref, mask_ref, win_ref, wgate_ref, wout_ref, gain_ref,
    dpair_ref, dwin_ref, dsmall_ref, dgain_ref, work, mix_out, mix_in, lr_out, lr_in, factor_out, factor_in, back_out, back_in,
    held, right_diag, left_cols, left_sums, right_sums, factors, slab_factors, slab_proj, proj,
    pairs_all, small_out, small_in, small_half, small_ring, small_mine, small_all,
    win_half, win_ring, win_mine, win_all,
    load_sems, save_sems, ring_send, ring_recv, send_sems, recv_sems, x_send, x_recv,
):
    row, col = lax.axis_index("row"), lax.axis_index("col")
    bank, z = row // RING, lax.rem(row, RING)
    me = bank * ACROSS + col
    core = lax.rem(col, 2)
    at_x, at_y = lax.rem(col // 2, 4), bank * 2 + col // 8

    def plane_id(peer):
        return ((peer // ACROSS) * RING + z, lax.rem(peer, ACROSS))

    def ring_id(place):
        return (bank * RING + place, col)

    def far_first(t):
        across, along, other = t // 8, lax.rem(t // 2, 4), 1 - lax.rem(t, 2)
        dy, dx = (3 - n + (2 * n - 1) * (1 - n // 2) for n in (across, along))
        return (
            lax.rem(at_y + dy, 4) * 8
            + lax.rem(at_x + dx, 4) * 2
            + lax.rem(core + other, 2)
        )

    plane_y = [lax.rem(at_y + n, 4) for n in range(4)]
    plane_row = [(y // 2) * RING + z for y in plane_y]
    plane_col = [lax.rem(y, 2) * 8 for y in plane_y]
    plane_x = [
        [lax.rem(at_x + n, 4) * 2 + lax.rem(core + other, 2) for other in range(2)]
        for n in range(4)
    ]

    barrier = pltpu.get_barrier_semaphore()

    @pl.loop(0, PLANE - 1)
    def _(t):
        pl.semaphore_signal(
            barrier, inc=1, device_id=plane_id(far_first(t)), device_id_type=MESH
        )

    for t in (1, RING - 1):
        pl.semaphore_signal(
            barrier, inc=1, device_id=ring_id(lax.rem(z + t, RING)), device_id_type=MESH
        )

    loads = [
        pltpu.make_async_copy(source, target, load_sems.at[k])
        for k, (source, target) in enumerate(
            [
                (pair_hbm, pair_ref), (wgate_hbm, wgate_ref), (grad_hbm, grad_ref),
                (wout_hbm, wout_ref), (hat_hbm, hat_ref), (gain_hbm, gain_ref),
                (rstd_hbm, rstd_ref), (win_hbm, win_ref), (mask_hbm, mask_ref),
            ]
        )
    ]
    for load in loads:
        load.start()

    saves = [
        pltpu.make_async_copy(source, target, save_sems.at[k])
        for k, (source, target) in enumerate(
            [
                (dpair_ref, dpair_hbm), (dwin_ref, dwin_hbm),
                (dsmall_ref, dsmall_hbm), (dgain_ref, dgain_hbm),
            ]
        )
    ]
    sent = []

    def plane_send(source, target, k):
        sent.append((target, PLANE, k))

        for across, along in ((a, b) for a in FAR_FIRST for b in FAR_FIRST):
            for other in (1, 0):
                if across or along or other:
                    peer = plane_y[across] * 8 + plane_x[along][other]
                    pltpu.make_async_remote_copy(
                        src_ref=source(peer), dst_ref=target.at[me],
                        send_sem=send_sems.at[k], recv_sem=recv_sems.at[k],
                        device_id=(plane_row[across], plane_col[across] + plane_x[along][other]),
                        device_id_type=MESH,
                    ).start()

    def ring_copy(source, target, offset, k):
        return pltpu.make_async_remote_copy(
            src_ref=source, dst_ref=target.at[z],
            send_sem=send_sems.at[k], recv_sem=recv_sems.at[k],
            device_id=ring_id(lax.rem(z + offset, RING)), device_id_type=MESH,
        )

    def ring_share(source, target, k, farthest=True):
        sent.append((target, RING, k))

        @pl.loop(0 if farthest else 1, RING - 1)
        def _(t):
            offset = RING // 2 + ((t + 1) // 2) * (2 * lax.rem(t + 1, 2) - 1)
            ring_copy(source, target, offset, k).start()

    def wait_bytes(ref, sem):
        pltpu.make_async_copy(ref, ref, sem).wait()

    def wait_many(target, count, k):
        wait_bytes(target.at[pl.ds(0, count - 1)], recv_sems.at[k])

    def start_hop(way, s, slot):
        hop(way, s, slot).start()

    def await_hop(way, s, slot):
        hop(way, s, slot).wait_recv()

    def settle():
        for target, count, k in sent:
            wait_bytes(target.at[pl.ds(0, count - 1)], send_sems.at[k])
        sent.clear()

    def hop(way, s, slot):
        step = 1 if way == 0 else RING - 1
        block = lax.rem(z + (RING - 1) * step * (s - 1), RING)
        return pltpu.make_async_remote_copy(
            src_ref=held.at[block, slot], dst_ref=held.at[block, slot],
            send_sem=ring_send.at[way], recv_sem=ring_recv.at[way, s - 1, slot],
            device_id=ring_id(lax.rem(z + step, RING)), device_id_type=MESH,
        )

    def piece(kind, first, second, turn):
        dy, dx = (second, first) if turn else (first, second)
        ty, tx = lax.rem(at_y + dy, 4), lax.rem(at_x + dx, 4)
        rows, k = pl.ds(0, ROWS), 40 + 4 * dy + dx
        to_y, to_x, to_core = at_y, at_x, 1 - core
        if kind != "core":
            way = 1 if kind[1] == "+" else 3
            far = first if kind[0] == "f" else second
            low, count = turn * ROWS // 2, ROWS // 2
            if far:
                low, count = low + (way // 2) * ROWS // 4, ROWS // 4
            rows = pl.ds(low, count)
            if (kind[0] == "f") == (turn == 0):
                to_y = lax.rem(at_y + way, 4)
            else:
                to_x = lax.rem(at_x + way, 4)
            to_core = core
            k = way // 2 + (2 if far else 0) + 20 * turn
            if kind[0] == "s":
                k += 4 + 4 * first
        place = pairs_all.at[ty // 2, rows, lax.rem(ty, 2) * 8 + tx * 2 + core]
        return pltpu.make_async_remote_copy(
            src_ref=place, dst_ref=place,
            send_sem=x_send.at[int(kind == "core")], recv_sem=x_recv.at[k],
            device_id=((to_y // 2) * RING + z, lax.rem(to_y, 2) * 8 + to_x * 2 + to_core),
            device_id_type=MESH,
        )

    def pass_on(kind, first, second, turn=0):
        piece(kind, first, second, turn).start()

    def take(kind, first, second, turn=0):
        piece(kind, first, second, turn).wait_recv()

    def relay(stage):
        if stage == 0:
            pairs_all[bank, :, col] = pair_ref[...]
        for turn in range(2):
            if stage == 0:
                for way in "+-":
                    pass_on("f" + way, 0, 0, turn)
                    pass_on("s" + way, 0, 0, turn)
            if stage == 1:
                for way, side in (("+", 3), ("-", 1)):
                    take("f" + way, 0, 0, turn)
                    pass_on("f" + way, side, 0, turn)
                    for to in "+-":
                        pass_on("s" + to, side, 0, turn)
                    take("s" + way, 0, 0, turn)
                    pass_on("s" + way, 0, side, turn)
            if stage == 2:
                take("f+", 3, 0, turn)
                take("f-", 1, 0, turn)
                for way in "+-":
                    pass_on("s" + way, 2, 0, turn)
                for first in (3, 1):
                    for way, side in (("+", 3), ("-", 1)):
                        take("s" + way, first, 0, turn)
                        pass_on("s" + way, first, side, turn)
                take("s+", 0, 3, turn)
                take("s-", 0, 1, turn)
            if stage == 3:
                for way, side in (("+", 3), ("-", 1)):
                    take("s" + way, 2, 0, turn)
                    pass_on("s" + way, 2, side, turn)
                for first in (3, 1):
                    take("s+", first, 3, turn)
                    take("s-", first, 1, turn)
            if stage == 4:
                take("s+", 2, 3, turn)
                take("s-", 2, 1, turn)
        for dy in range(4):
            for dx in range(4):
                if stage == min(dy, 4 - dy) + min(dx, 4 - dx):
                    pass_on("core", dy, dx)
                if stage in (5, 6) and (stage == 6) == (2 in (dy, dx)):
                    take("core", dy, dx)

    def column(values):
        return jnp.sum(jnp.where(diagonal, values, 0.0), axis=1, keepdims=True)

    diagonal = lax.broadcasted_iota(jnp.int32, (WIDTH, WIDTH), 0) == lax.broadcasted_iota(
        jnp.int32, (WIDTH, WIDTH), 1
    )
    for load in loads[:3]:
        load.wait()
    x = pair_ref[...].reshape(PAIRS, WIDTH)
    gate = jax.nn.sigmoid(mm(wgate_ref[...], x, 0, 1))
    grad = grad_ref[...].reshape(PAIRS, WIDTH).astype(F32).T
    gated = (grad * gate).astype(BF16)
    for load in loads[3:7]:
        load.wait()
    scaled_grad = mm(wout_ref[...], gated, 1, 0)
    hat = hat_ref[...].reshape(PAIRS, WIDTH).astype(F32).T
    gain = column(gain_ref[...])
    spread = jnp.concatenate([rstd_ref[...]] * ROWS, axis=1)
    own_row = lax.broadcasted_iota(jnp.int32, (1, PAIRS), 1) // COLS
    own_row = own_row == lax.broadcasted_iota(jnp.int32, spread.shape, 0)
    rstd = jnp.sum(jnp.where(own_row, spread, 0.0), axis=0, keepdims=True)
    h = scaled_grad * gain
    mean_h = jnp.mean(h, axis=0, keepdims=True)
    mean_hx = jnp.mean(h * hat, axis=0, keepdims=True)
    mix = rstd * (h - mean_h - hat * mean_hx)
    mix_out[...] = to_tiles(mix, work)
    mix_in[me] = mix_out[me]
    for load in loads[7:]:
        load.wait()
    pl.semaphore_wait(barrier, PLANE + 1)
    plane_send(lambda peer: mix_out.at[peer], mix_in, 0)

    token = lax.broadcasted_iota(jnp.int32, (TOKENS, PAIRS), 0)
    pair = lax.broadcasted_iota(jnp.int32, (1, PAIRS), 1)
    mask = jnp.broadcast_to(mask_ref[...].astype(F32), (8, TOKENS)).astype(BF16)
    one_hot = lambda place: jnp.where(token == place, 1.0, 0.0).astype(BF16)
    mask_row = mm(mask, one_hot(row * ROWS + pair // COLS), 1, 0)
    mask_col = mm(mask, one_hot(col * COLS + lax.rem(pair, COLS)), 1, 0)
    pair_mask = (mask_row * mask_col)[:1]
    projected = mm(win_ref[...], x, 0, 1)
    value_a, logit_a = projected[:WIDTH], projected[WIDTH : 2 * WIDTH]
    value_b, logit_b = projected[2 * WIDTH : 3 * WIDTH], projected[3 * WIDTH :]
    sigma_a, sigma_b = jax.nn.sigmoid(logit_a), jax.nn.sigmoid(logit_b)
    masked_a, masked_b = pair_mask * sigma_a, pair_mask * sigma_b
    lr_out[:, :ROWS] = to_tiles(masked_a * value_a, work)
    lr_out[:, ROWS:] = to_tiles(masked_b * value_b, work)
    lr_in[me] = lr_out[me]
    plane_send(lambda peer: lr_out.at[peer], lr_in, 1)
    factors[0] = masked_a
    factors[1] = masked_a * value_a * (1.0 - sigma_a)
    factors[2] = masked_b
    factors[3] = masked_b * value_b * (1.0 - sigma_b)

    scaled = (hat * gain).astype(BF16)
    output = mm(wout_ref[...], scaled, 0, 0)
    gate_grad = (grad * output * gate * (1.0 - gate)).astype(BF16)
    proj[4 * WIDTH :] = gate_grad
    squares = [mm(x, gate_grad, 0, 1), mm(scaled, gated, 1, 1)]
    squares = jnp.concatenate(squares, axis=0).reshape(PLANE, 8, WIDTH)
    part_gain = jnp.sum(scaled_grad * hat, axis=1, keepdims=True)
    part_gain = jnp.sum(jnp.where(diagonal, part_gain, 0.0), axis=0, keepdims=True)
    part_gain = jnp.broadcast_to(part_gain[None], (PLANE, 8, WIDTH))
    small_out[...] = jnp.concatenate([squares, part_gain], axis=1).astype(BF16)
    small_in[me] = small_out[me]

    wait_many(mix_in, PLANE, 0)
    slab = gather_slab(mix_in[...]).astype(BF16)
    for slot in range(SLOTS):
        held[z, slot] = slab[slot * BANKS * ROWS : (slot + 1) * BANKS * ROWS]
        for way in range(2):
            start_hop(way, 1, slot)


    wait_many(lr_in, PLANE, 1)
    left_cols[...] = gather_slab(lr_in[:, :ROWS]).T.astype(BF16)
    right = gather_slab(lr_in[:, ROWS:]).astype(BF16)
    right_diag[...] = jnp.zeros_like(right_diag)
    for slot in range(SLOTS):
        rows = slice(slot * BANKS * ROWS, (slot + 1) * BANKS * ROWS)
        right_diag[rows, slot * TOKENS : (slot + 1) * TOKENS] = right[rows]
    right_sums[...] = jnp.zeros_like(right_sums)

    def contract(blocks):
        mixes = [
            jnp.concatenate([held[block, slot] for block in blocks], axis=0)
            for slot in range(SLOTS)
        ]
        places = [
            pl.ds(pl.multiple_of(b * (TOKENS // BANKS) + block * ROWS, ROWS), ROWS)
            for block in blocks
            for b in range(BANKS)
        ]
        sums = mm(jnp.concatenate(mixes, axis=1), right_diag[...], 1, 1)
        for n, place in enumerate(places):
            left_sums[place] = sums[n * ROWS : (n + 1) * ROWS]
        lefts = jnp.concatenate([left_cols[place] for place in places], axis=0).astype(F32)
        lefts = lefts.T.astype(BF16)
        for slot in range(SLOTS):
            rows = slice(slot * BANKS * ROWS, (slot + 1) * BANKS * ROWS)
            right_sums[rows] += mm(lefts[rows], mixes[slot], 1, 0)

    def ring_step(s, last):
        for slot in range(SLOTS):
            for way in range(2):
                await_hop(way, s, slot)
                if not last or way == slot // 2:
                    start_hop(way, s + 1, slot)
        contract([lax.rem(z + RING - s, RING), lax.rem(z + s, RING)])

    contract([z])
    relay(0)
    ring_step(1, False)
    factor_out[:, 0 * ROWS : 1 * ROWS] = to_tiles(factors[0], work)
    factor_out[:, 1 * ROWS : 2 * ROWS] = to_tiles(factors[1], work)
    factor_out[:, 2 * ROWS : 3 * ROWS] = to_tiles(factors[2], work)
    factor_out[:, 3 * ROWS : 4 * ROWS] = to_tiles(factors[3], work)
    ring_step(2, False)
    factor_in[me] = factor_out[me]
    plane_send(lambda peer: factor_out.at[peer], factor_in, 2)
    ring_step(3, False)
    relay(1)
    plane_send(lambda peer: small_out.at[peer], small_in, 3)
    ring_step(4, False)
    ring_step(5, False)
    relay(2)
    wait_many(factor_in, PLANE, 2)
    slab_factors[0] = gather_slab(factor_in[:, 0 * ROWS : 1 * ROWS]).astype(BF16)
    slab_factors[1] = gather_slab(factor_in[:, 1 * ROWS : 2 * ROWS]).astype(BF16)
    slab_factors[2] = gather_slab(factor_in[:, 2 * ROWS : 3 * ROWS]).astype(BF16)
    slab_factors[3] = gather_slab(factor_in[:, 3 * ROWS : 4 * ROWS]).astype(BF16)
    ring_step(6, False)
    relay(3)
    wait_many(small_in, PLANE, 3)
    small_half[...] = jnp.sum(small_in[...].astype(F32), axis=0).astype(BF16)
    small_ring[z] = small_half[...]
    ring_step(7, True)
    ring_share(small_half, small_ring, 4, False)
    relay(4)
    for slot in range(SLOTS):
        await_hop(slot // 2, RING // 2, slot)
    ring_copy(small_half, small_ring, RING // 2, 4).start()
    contract([lax.rem(z + RING // 2, RING)])
    relay(5)

    left_grad = left_sums[...].T
    for n in range(2):
        values = left_grad if n == 0 else right_sums[...]
        values = values.astype(BF16).astype(F32)
        for m in range(2):
            terms = values * slab_factors[2 * n + m].astype(F32)
            for g in range(4):
                slab_proj[g, (2 * n + m) * WIDTH : (2 * n + m + 1) * WIDTH] = terms[
                    :, g * 128 : (g + 1) * 128
                ]
    relay(6)
    total = jnp.zeros((4 * SLOTS, WIDTH), F32)
    for k in range(BANKS * ROWS):
        terms = jnp.concatenate(
            [slab_proj[g, pl.ds(k, 4 * SLOTS, stride=BANKS * ROWS), :] for g in range(4)], axis=1
        )
        pairs = pairs_all[k // ROWS, k % ROWS].reshape(TOKENS, WIDTH)
        total = total + mm(terms.astype(BF16), pairs, 1, 0)
    win_half[...] = total.astype(BF16)
    win_ring[z] = win_half[...]
    ring_share(win_half, win_ring, 5)

    back_out[:, :ROWS] = scatter_slab(left_grad)
    back_out[:, ROWS:] = scatter_slab(right_sums[...])
    back_in[me] = back_out[me]
    plane_send(lambda peer: back_out.at[peer], back_in, 6)

    def ring_total(ring):
        return jnp.sum(ring[...].astype(F32), axis=0) * (1.0 / TOKENS)

    wait_many(small_ring, RING, 4)
    small_mine[...] = ring_total(small_ring)
    dgain_ref[...] = small_mine[8:9]
    saves[3].start()
    small_all[me] = small_mine[:8]
    plane_send(lambda peer: small_mine.at[pl.ds(0, 8)], small_all, 7)

    settle()
    for way in range(2):
        wait_bytes(held.at[pl.ds(0, RING - 1), pl.ds(0, 2)], ring_send.at[way])
    wait_bytes(pairs_all.at[0, :, pl.ds(0, ACROSS - 1)], x_send.at[0])
    wait_bytes(pairs_all.at[0], x_send.at[1])
    wait_many(win_ring, RING, 5)
    win_mine[...] = ring_total(win_ring).astype(BF16)
    win_all[me] = win_mine[...]
    plane_send(lambda peer: win_mine, win_all, 8)

    wait_many(back_in, PLANE, 6)
    grad_left = from_tiles(back_in[:, :ROWS], work)
    proj[:WIDTH] = (grad_left * factors[0]).astype(BF16)
    proj[WIDTH : 2 * WIDTH] = (grad_left * factors[1]).astype(BF16)
    grad_right = from_tiles(back_in[:, ROWS:], work)
    proj[2 * WIDTH : 3 * WIDTH] = (grad_right * factors[2]).astype(BF16)
    proj[3 * WIDTH : 4 * WIDTH] = (grad_right * factors[3]).astype(BF16)
    weights = jnp.concatenate([win_ref[...], wgate_ref[...]], axis=1)
    d_pair = mm(weights, proj[...], 1, 0)
    dpair_ref[...] = d_pair.T.astype(BF16).reshape(ROWS, COLS, WIDTH)
    saves[0].start()

    wait_many(small_all, PLANE, 7)
    dsmall_ref[...] = small_all[...].reshape(2 * WIDTH, WIDTH)
    saves[2].start()
    wait_many(win_all, PLANE, 8)
    work[...] = win_all[...].astype(F32).reshape(4 * WIDTH, WIDTH)
    dwin_ref[...] = jnp.concatenate(
        [work[pl.ds(n, PLANE, stride=4 * SLOTS), :] for n in range(4 * SLOTS)], axis=0
    ).T
    saves[1].start()
    settle()
    for save in saves:
        save.wait()


def finish(dpair, dwin, dsmall, dgain, dpair_out, dwin_out, dwgate_out, dwout_out, dgain_out, *rest):
    held, loads, saves = rest[:4], rest[4], rest[5]
    sources = [dpair, dwin, dsmall, dgain]
    first = [
        pltpu.make_async_copy(source, target, loads.at[k])
        for k, (source, target) in enumerate(zip(sources, held))
    ]
    last = [
        pltpu.make_async_copy(source, target, saves.at[k])
        for k, (source, target) in enumerate(
            [
                (held[0], dpair_out),
                (held[1], dwin_out),
                (held[2].at[pl.ds(0, WIDTH)], dwgate_out),
                (held[2].at[pl.ds(WIDTH, WIDTH)], dwout_out),
                (held[3], dgain_out),
            ]
        )
    ]
    for copy in first:
        copy.start()
    for k, copies in enumerate([last[:1], last[1:2], last[2:4], last[4:]]):
        first[k].wait()
        for copy in copies:
            copy.start()
    for copy in last:
        copy.wait()


def shards(pair_norm, out_hat, out_rstd, grad_out, token_mask, w_in, w_gate, w_out, ln_gain):
    tile = (ROWS, COLS, WIDTH)
    square = (WIDTH, WIDTH)
    hbm = pl.BlockSpec(memory_space=pltpu.HBM)
    shape = jax.ShapeDtypeStruct
    tiles = lambda rows, dtype: pltpu.VMEM((PLANE, rows, WIDTH), dtype)
    results = pl.pallas_call(
        kernel,
        out_shape=(
            shape(tile, BF16),
            shape((WIDTH, 4 * WIDTH), F32),
            shape((2 * WIDTH, WIDTH), F32),
            shape((1, WIDTH), F32),
        ),
        in_specs=[hbm] * 9,
        out_specs=[hbm] * 4,
        scratch_shapes=[
            pltpu.VMEM(tile, BF16),
            pltpu.VMEM(tile, BF16),
            pltpu.VMEM((ROWS, COLS), F32),
            pltpu.VMEM(tile, BF16),
            pltpu.VMEM((1, TOKENS), jnp.int32),
            pltpu.VMEM((WIDTH, 4 * WIDTH), BF16),
            pltpu.VMEM(square, BF16),
            pltpu.VMEM(square, BF16),
            pltpu.VMEM((1, WIDTH), F32),
            pltpu.VMEM(tile, BF16),
            pltpu.VMEM((WIDTH, 4 * WIDTH), F32),
            pltpu.VMEM((2 * WIDTH, WIDTH), F32),
            pltpu.VMEM((1, WIDTH), F32),
            pltpu.VMEM((PAIRS, WIDTH), F32),
            *[tiles(ROWS, BF16)] * 2,
            *[tiles(2 * ROWS, BF16)] * 2,
            *[tiles(4 * ROWS, BF16)] * 2,
            *[tiles(2 * ROWS, BF16)] * 2,
            pltpu.VMEM((RING, SLOTS, BANKS * ROWS, TOKENS), BF16),
            pltpu.VMEM((WIDTH, SLOTS * TOKENS), BF16),
            pltpu.VMEM((TOKENS, WIDTH), BF16),
            pltpu.VMEM((TOKENS, WIDTH), F32),
            pltpu.VMEM((WIDTH, TOKENS), F32),
            pltpu.VMEM((4, WIDTH, PAIRS), F32),
            pltpu.VMEM((4, WIDTH, TOKENS), BF16),
            pltpu.VMEM((4, 4 * WIDTH, 128), F32),
            pltpu.VMEM((5 * WIDTH, PAIRS), BF16),
            pltpu.VMEM((BANKS, ROWS, ACROSS, COLS, WIDTH), BF16),
            tiles(ROWS, BF16),
            tiles(ROWS, BF16),
            pltpu.VMEM((ROWS, WIDTH), BF16),
            pltpu.VMEM((RING, ROWS, WIDTH), BF16),
            pltpu.VMEM((ROWS, WIDTH), F32),
            tiles(8, F32),
            pltpu.VMEM((ROWS, WIDTH), BF16),
            pltpu.VMEM((RING, ROWS, WIDTH), BF16),
            pltpu.VMEM((ROWS, WIDTH), BF16),
            tiles(ROWS, BF16),
            pltpu.SemaphoreType.DMA((9,)),
            pltpu.SemaphoreType.DMA((4,)),
            pltpu.SemaphoreType.DMA((2,)),
            pltpu.SemaphoreType.DMA((2, RING // 2, SLOTS)),
            pltpu.SemaphoreType.DMA((9,)),
            pltpu.SemaphoreType.DMA((9,)),
            pltpu.SemaphoreType.DMA((2,)),
            pltpu.SemaphoreType.DMA((56,)),
        ],
        compiler_params=pltpu.CompilerParams(
            collective_id=0, has_side_effects=True, vmem_limit_bytes=62 * 1024 * 1024
        ),
    )(
        pair_norm, out_hat, out_rstd, grad_out, token_mask.reshape(1, TOKENS),
        w_in, w_gate, w_out, ln_gain.reshape(1, WIDTH),
    )
    d_pair, d_win, d_wgate, d_wout, d_gain = pl.pallas_call(
        finish,
        out_shape=(
            shape(tile, BF16),
            shape((WIDTH, 4 * WIDTH), F32),
            shape(square, F32),
            shape(square, F32),
            shape((1, WIDTH), F32),
        ),
        in_specs=[hbm] * 4,
        out_specs=[hbm] * 5,
        scratch_shapes=[
            pltpu.VMEM(tile, BF16),
            pltpu.VMEM((WIDTH, 4 * WIDTH), F32),
            pltpu.VMEM((2 * WIDTH, WIDTH), F32),
            pltpu.VMEM((1, WIDTH), F32),
            pltpu.SemaphoreType.DMA((4,)),
            pltpu.SemaphoreType.DMA((5,)),
        ],
        compiler_params=pltpu.CompilerParams(vmem_limit_bytes=62 * 1024 * 1024),
    )(*results)
    return d_pair, d_win, d_wgate, d_wout, d_gain.reshape(WIDTH)


def solution(mesh):
    tile = P("row", "col", None)
    in_specs = (tile, tile, P("row", "col"), tile, P(), P(), P(), P(), P())
    out_specs = (tile, P(), P(), P(), P())
    return jax.shard_map(shards, mesh=mesh, in_specs=in_specs, out_specs=out_specs, check_vma=False)
```

```python
import jax
import jax.numpy as jnp
from jax import lax
from jax.experimental import pallas as pl
from jax.experimental.pallas import tpu as pltpu
from jax.sharding import PartitionSpec as P

F32, BF16 = jnp.float32, jnp.bfloat16
MESH = pl.DeviceIdType.MESH

TOKENS = 512
WIDTH = 128
ROWS, COLS = 16, 32
PAIRS = ROWS * COLS
RING = 16
BANKS = 2
ACROSS = 16
PLANE = BANKS * ACROSS
SLOTS = WIDTH // PLANE
CHUNK = 128 // SLOTS
FAR_FIRST = (2, 3, 1, 0)


def mm(a, b, ca, cb):
    return lax.dot_general(a, b, (((ca,), (cb,)), ((), ())), preferred_element_type=F32)


def swap_chunks(parts):
    lane = lax.broadcasted_iota(jnp.int32, parts[0].shape, 1)
    low = lane < 64
    even = lax.rem(lane // CHUNK, 2) == 0
    a, b, c, d = parts
    a, c = jnp.where(low, a, pltpu.roll(c, 64, 1)), jnp.where(low, pltpu.roll(a, 64, 1), c)
    b, d = jnp.where(low, b, pltpu.roll(d, 64, 1)), jnp.where(low, pltpu.roll(b, 64, 1), d)
    a, b = jnp.where(even, a, pltpu.roll(b, 32, 1)), jnp.where(even, pltpu.roll(a, 96, 1), b)
    c, d = jnp.where(even, c, pltpu.roll(d, 32, 1)), jnp.where(even, pltpu.roll(c, 96, 1), d)
    return a, b, c, d


def to_tiles(values, work):
    parts = []
    for slot in range(SLOTS):
        block = values[slot * PLANE : (slot + 1) * PLANE]
        parts.append(jnp.concatenate([block[:, g * 128 : (g + 1) * 128] for g in range(4)], axis=0))
    for low, part in enumerate(swap_chunks(parts)):
        for g in range(4):
            work[pl.ds(4 * g + low, PLANE, stride=ROWS), :] = part[g * PLANE : (g + 1) * PLANE]
    return work[...].astype(BF16).reshape(PLANE, ROWS, 128)


def from_tiles(tiles, work):
    work[...] = tiles.astype(F32).reshape(PLANE * ROWS, 128)
    parts = []
    for low in range(4):
        parts.append(
            jnp.concatenate(
                [work[pl.ds(4 * g + low, PLANE, stride=ROWS), :] for g in range(4)], axis=0
            )
        )
    out = []
    for part in swap_chunks(parts):
        out.append(
            jnp.concatenate([part[g * PLANE : (g + 1) * PLANE] for g in range(4)], axis=1)
        )
    return jnp.concatenate(out, axis=0)


def gather_slab(tiles):
    tiles = tiles.astype(F32).reshape(BANKS, 4, 4, ROWS, 128)
    parts = [tiles[:, :, q].reshape(BANKS * 4 * ROWS, 128) for q in range(4)]
    out = []
    for part in swap_chunks(parts):
        part = part.reshape(BANKS, 4, ROWS, 128)
        out.append(
            jnp.concatenate([part[:, g].reshape(BANKS * ROWS, 128) for g in range(4)], axis=1)
        )
    return jnp.concatenate(out, axis=0)


def scatter_slab(slab):
    parts = []
    for slot in range(SLOTS):
        block = slab[slot * BANKS * ROWS : (slot + 1) * BANKS * ROWS]
        block = [
            block[:, g * 128 : (g + 1) * 128].reshape(BANKS, 1, ROWS, 128) for g in range(4)
        ]
        parts.append(jnp.concatenate(block, axis=1).reshape(BANKS * 4 * ROWS, 128))
    out = [
        part.reshape(BANKS, 4, 1, ROWS, 128) for part in swap_chunks(parts)
    ]
    return jnp.concatenate(out, axis=2).reshape(PLANE, ROWS, 128).astype(BF16)


def kernel(
    pair_hbm, hat_hbm, rstd_hbm, grad_hbm, mask_hbm, win_hbm, wgate_hbm, wout_hbm, gain_hbm,
    dpair_hbm, dwin_hbm, dsmall_hbm, dgain_hbm,
    pair_ref, hat_ref, rstd_ref, grad_ref, mask_ref, win_ref, wgate_ref, wout_ref, gain_ref,
    dpair_ref, dwin_ref, dsmall_ref, dgain_ref, work, mix_out, mix_in, lr_out, lr_in, factor_out, factor_in, back_out, back_in,
    held, right_diag, left_cols, left_sums, right_sums, factors, slab_factors, slab_proj, proj,
    pairs_all, small_out, small_in, small_half, small_ring, small_mine, small_all,
    win_half, win_ring, win_mine, win_all,
    load_sems, save_sems, ring_send, ring_recv, send_sems, recv_sems, x_send, x_recv,
):
    row, col = lax.axis_index("row"), lax.axis_index("col")
    bank, z = row // RING, lax.rem(row, RING)
    me = bank * ACROSS + col
    core = lax.rem(col, 2)
    at_x, at_y = lax.rem(col // 2, 4), bank * 2 + col // 8

    def plane_id(peer):
        return ((peer // ACROSS) * RING + z, lax.rem(peer, ACROSS))

    def ring_id(place):
        return (bank * RING + place, col)

    def far_first(t):
        across, along, other = t // 8, lax.rem(t // 2, 4), 1 - lax.rem(t, 2)
        dy, dx = (3 - n + (2 * n - 1) * (1 - n // 2) for n in (across, along))
        return (
            lax.rem(at_y + dy, 4) * 8
            + lax.rem(at_x + dx, 4) * 2
            + lax.rem(core + other, 2)
        )

    plane_y = [lax.rem(at_y + n, 4) for n in range(4)]
    plane_row = [(y // 2) * RING + z for y in plane_y]
    plane_col = [lax.rem(y, 2) * 8 for y in plane_y]
    plane_x = [
        [lax.rem(at_x + n, 4) * 2 + lax.rem(core + other, 2) for other in range(2)]
        for n in range(4)
    ]

    barrier = pltpu.get_barrier_semaphore()

    @pl.loop(0, PLANE - 1)
    def _(t):
        pl.semaphore_signal(
            barrier, inc=1, device_id=plane_id(far_first(t)), device_id_type=MESH
        )

    for t in (1, RING - 1):
        pl.semaphore_signal(
            barrier, inc=1, device_id=ring_id(lax.rem(z + t, RING)), device_id_type=MESH
        )

    loads = [
        pltpu.make_async_copy(source, target, load_sems.at[k])
        for k, (source, target) in enumerate(
            [
                (pair_hbm, pair_ref), (wgate_hbm, wgate_ref), (grad_hbm, grad_ref),
                (wout_hbm, wout_ref), (hat_hbm, hat_ref), (gain_hbm, gain_ref),
                (rstd_hbm, rstd_ref), (win_hbm, win_ref), (mask_hbm, mask_ref),
            ]
        )
    ]
    for load in loads:
        load.start()

    saves = [
        pltpu.make_async_copy(source, target, save_sems.at[k])
        for k, (source, target) in enumerate(
            [
                (dpair_ref, dpair_hbm), (dwin_ref, dwin_hbm),
                (dsmall_ref, dsmall_hbm), (dgain_ref, dgain_hbm),
            ]
        )
    ]
    sent = []

    def plane_send(source, target, k):
        sent.append((target, PLANE, k))

        for across, along in ((a, b) for a in FAR_FIRST for b in FAR_FIRST):
            for other in (1, 0):
                if across or along or other:
                    peer = plane_y[across] * 8 + plane_x[along][other]
                    pltpu.make_async_remote_copy(
                        src_ref=source(peer), dst_ref=target.at[me],
                        send_sem=send_sems.at[k], recv_sem=recv_sems.at[k],
                        device_id=(plane_row[across], plane_col[across] + plane_x[along][other]),
                        device_id_type=MESH,
                    ).start()

    def ring_copy(source, target, offset, k):
        return pltpu.make_async_remote_copy(
            src_ref=source, dst_ref=target.at[z],
            send_sem=send_sems.at[k], recv_sem=recv_sems.at[k],
            device_id=ring_id(lax.rem(z + offset, RING)), device_id_type=MESH,
        )

    def ring_share(source, target, k, farthest=True):
        sent.append((target, RING, k))

        @pl.loop(0 if farthest else 1, RING - 1)
        def _(t):
            offset = RING // 2 + ((t + 1) // 2) * (2 * lax.rem(t + 1, 2) - 1)
            ring_copy(source, target, offset, k).start()

    def wait_bytes(ref, sem):
        pltpu.make_async_copy(ref, ref, sem).wait()

    def wait_many(target, count, k):
        wait_bytes(target.at[pl.ds(0, count - 1)], recv_sems.at[k])

    def start_hop(way, s, slot):
        hop(way, s, slot).start()

    def await_hop(way, s, slot):
        hop(way, s, slot).wait_recv()

    def settle():
        for target, count, k in sent:
            wait_bytes(target.at[pl.ds(0, count - 1)], send_sems.at[k])
        sent.clear()

    def hop(way, s, slot):
        step = 1 if way == 0 else RING - 1
        block = lax.rem(z + (RING - 1) * step * (s - 1), RING)
        return pltpu.make_async_remote_copy(
            src_ref=held.at[block, slot], dst_ref=held.at[block, slot],
            send_sem=ring_send.at[way], recv_sem=ring_recv.at[way, s - 1, slot],
            device_id=ring_id(lax.rem(z + step, RING)), device_id_type=MESH,
        )

    def piece(kind, first, second, turn):
        dy, dx = (second, first) if turn else (first, second)
        ty, tx = lax.rem(at_y + dy, 4), lax.rem(at_x + dx, 4)
        rows, k = pl.ds(0, ROWS), 40 + 4 * dy + dx
        to_y, to_x, to_core = at_y, at_x, 1 - core
        if kind != "core":
            way = 1 if kind[1] == "+" else 3
            far = first if kind[0] == "f" else second
            low, count = turn * ROWS // 2, ROWS // 2
            if far:
                low, count = low + (way // 2) * ROWS // 4, ROWS // 4
            rows = pl.ds(low, count)
            if (kind[0] == "f") == (turn == 0):
                to_y = lax.rem(at_y + way, 4)
            else:
                to_x = lax.rem(at_x + way, 4)
            to_core = core
            k = way // 2 + (2 if far else 0) + 20 * turn
            if kind[0] == "s":
                k += 4 + 4 * first
        place = pairs_all.at[ty // 2, rows, lax.rem(ty, 2) * 8 + tx * 2 + core]
        return pltpu.make_async_remote_copy(
            src_ref=place, dst_ref=place,
            send_sem=x_send.at[int(kind == "core")], recv_sem=x_recv.at[k],
            device_id=((to_y // 2) * RING + z, lax.rem(to_y, 2) * 8 + to_x * 2 + to_core),
            device_id_type=MESH,
        )

    def pass_on(kind, first, second, turn=0):
        piece(kind, first, second, turn).start()

    def take(kind, first, second, turn=0):
        piece(kind, first, second, turn).wait_recv()

    def relay(stage):
        if stage == 0:
            pairs_all[bank, :, col] = pair_ref[...]
        for turn in range(2):
            if stage == 0:
                for way in "+-":
                    pass_on("f" + way, 0, 0, turn)
                    pass_on("s" + way, 0, 0, turn)
            if stage == 1:
                for way, side in (("+", 3), ("-", 1)):
                    take("f" + way, 0, 0, turn)
                    pass_on("f" + way, side, 0, turn)
                    for to in "+-":
                        pass_on("s" + to, side, 0, turn)
                    take("s" + way, 0, 0, turn)
                    pass_on("s" + way, 0, side, turn)
            if stage == 2:
                take("f+", 3, 0, turn)
                take("f-", 1, 0, turn)
                for way in "+-":
                    pass_on("s" + way, 2, 0, turn)
                for first in (3, 1):
                    for way, side in (("+", 3), ("-", 1)):
                        take("s" + way, first, 0, turn)
                        pass_on("s" + way, first, side, turn)
                take("s+", 0, 3, turn)
                take("s-", 0, 1, turn)
            if stage == 3:
                for way, side in (("+", 3), ("-", 1)):
                    take("s" + way, 2, 0, turn)
                    pass_on("s" + way, 2, side, turn)
                for first in (3, 1):
                    take("s+", first, 3, turn)
                    take("s-", first, 1, turn)
            if stage == 4:
                take("s+", 2, 3, turn)
                take("s-", 2, 1, turn)
        for dy in range(4):
            for dx in range(4):
                if stage == min(dy, 4 - dy) + min(dx, 4 - dx):
                    pass_on("core", dy, dx)
                if stage in (5, 6) and (stage == 6) == (2 in (dy, dx)):
                    take("core", dy, dx)

    def column(values):
        return jnp.sum(jnp.where(diagonal, values, 0.0), axis=1, keepdims=True)

    diagonal = lax.broadcasted_iota(jnp.int32, (WIDTH, WIDTH), 0) == lax.broadcasted_iota(
        jnp.int32, (WIDTH, WIDTH), 1
    )
    for load in loads[:3]:
        load.wait()
    x = pair_ref[...].reshape(PAIRS, WIDTH)
    gate = jax.nn.sigmoid(mm(wgate_ref[...], x, 0, 1))
    grad = grad_ref[...].reshape(PAIRS, WIDTH).astype(F32).T
    gated = (grad * gate).astype(BF16)
    for load in loads[3:7]:
        load.wait()
    scaled_grad = mm(wout_ref[...], gated, 1, 0)
    hat = hat_ref[...].reshape(PAIRS, WIDTH).astype(F32).T
    gain = column(gain_ref[...])
    spread = jnp.concatenate([rstd_ref[...]] * ROWS, axis=1)
    own_row = lax.broadcasted_iota(jnp.int32, (1, PAIRS), 1) // COLS
    own_row = own_row == lax.broadcasted_iota(jnp.int32, spread.shape, 0)
    rstd = jnp.sum(jnp.where(own_row, spread, 0.0), axis=0, keepdims=True)
    h = scaled_grad * gain
    mean_h = jnp.mean(h, axis=0, keepdims=True)
    mean_hx = jnp.mean(h * hat, axis=0, keepdims=True)
    mix = rstd * (h - mean_h - hat * mean_hx)
    mix_out[...] = to_tiles(mix, work)
    mix_in[me] = mix_out[me]
    for load in loads[7:]:
        load.wait()
    pl.semaphore_wait(barrier, PLANE + 1)
    plane_send(lambda peer: mix_out.at[peer], mix_in, 0)

    token = lax.broadcasted_iota(jnp.int32, (TOKENS, PAIRS), 0)
    pair = lax.broadcasted_iota(jnp.int32, (1, PAIRS), 1)
    mask = jnp.broadcast_to(mask_ref[...].astype(F32), (8, TOKENS)).astype(BF16)
    one_hot = lambda place: jnp.where(token == place, 1.0, 0.0).astype(BF16)
    mask_row = mm(mask, one_hot(row * ROWS + pair // COLS), 1, 0)
    mask_col = mm(mask, one_hot(col * COLS + lax.rem(pair, COLS)), 1, 0)
    pair_mask = (mask_row * mask_col)[:1]
    projected = mm(win_ref[...], x, 0, 1)
    value_a, logit_a = projected[:WIDTH], projected[WIDTH : 2 * WIDTH]
    value_b, logit_b = projected[2 * WIDTH : 3 * WIDTH], projected[3 * WIDTH :]
    sigma_a, sigma_b = jax.nn.sigmoid(logit_a), jax.nn.sigmoid(logit_b)
    masked_a, masked_b = pair_mask * sigma_a, pair_mask * sigma_b
    lr_out[:, :ROWS] = to_tiles(masked_a * value_a, work)
    lr_out[:, ROWS:] = to_tiles(masked_b * value_b, work)
    lr_in[me] = lr_out[me]
    plane_send(lambda peer: lr_out.at[peer], lr_in, 1)
    factors[0] = masked_a
    factors[1] = masked_a * value_a * (1.0 - sigma_a)
    factors[2] = masked_b
    factors[3] = masked_b * value_b * (1.0 - sigma_b)

    scaled = (hat * gain).astype(BF16)
    output = mm(wout_ref[...], scaled, 0, 0)
    gate_grad = (grad * output * gate * (1.0 - gate)).astype(BF16)
    proj[4 * WIDTH :] = gate_grad
    squares = [mm(x, gate_grad, 0, 1), mm(scaled, gated, 1, 1)]
    squares = jnp.concatenate(squares, axis=0).reshape(PLANE, 8, WIDTH)
    part_gain = jnp.sum(scaled_grad * hat, axis=1, keepdims=True)
    part_gain = jnp.sum(jnp.where(diagonal, part_gain, 0.0), axis=0, keepdims=True)
    part_gain = jnp.broadcast_to(part_gain[None], (PLANE, 8, WIDTH))
    small_out[...] = jnp.concatenate([squares, part_gain], axis=1).astype(BF16)
    small_in[me] = small_out[me]

    wait_many(mix_in, PLANE, 0)
    slab = gather_slab(mix_in[...]).astype(BF16)
    for slot in range(SLOTS):
        held[z, slot] = slab[slot * BANKS * ROWS : (slot + 1) * BANKS * ROWS]
        for way in range(2):
            start_hop(way, 1, slot)


    wait_many(lr_in, PLANE, 1)
    left_cols[...] = gather_slab(lr_in[:, :ROWS]).T.astype(BF16)
    right = gather_slab(lr_in[:, ROWS:]).astype(BF16)
    right_diag[...] = jnp.zeros_like(right_diag)
    for slot in range(SLOTS):
        rows = slice(slot * BANKS * ROWS, (slot + 1) * BANKS * ROWS)
        right_diag[rows, slot * TOKENS : (slot + 1) * TOKENS] = right[rows]
    right_sums[...] = jnp.zeros_like(right_sums)

    def contract(blocks):
        mixes = [
            jnp.concatenate([held[block, slot] for block in blocks], axis=0)
            for slot in range(SLOTS)
        ]
        places = [
            pl.ds(pl.multiple_of(b * (TOKENS // BANKS) + block * ROWS, ROWS), ROWS)
            for block in blocks
            for b in range(BANKS)
        ]
        sums = mm(jnp.concatenate(mixes, axis=1), right_diag[...], 1, 1)
        for n, place in enumerate(places):
            left_sums[place] = sums[n * ROWS : (n + 1) * ROWS]
        lefts = jnp.concatenate([left_cols[place] for place in places], axis=0).astype(F32)
        lefts = lefts.T.astype(BF16)
        for slot in range(SLOTS):
            rows = slice(slot * BANKS * ROWS, (slot + 1) * BANKS * ROWS)
            right_sums[rows] += mm(lefts[rows], mixes[slot], 1, 0)

    def ring_step(s, last):
        for slot in range(SLOTS):
            for way in range(2):
                await_hop(way, s, slot)
                if not last or way == slot // 2:
                    start_hop(way, s + 1, slot)
        contract([lax.rem(z + RING - s, RING), lax.rem(z + s, RING)])

    contract([z])
    relay(0)
    ring_step(1, False)
    factor_out[:, 0 * ROWS : 1 * ROWS] = to_tiles(factors[0], work)
    factor_out[:, 1 * ROWS : 2 * ROWS] = to_tiles(factors[1], work)
    factor_out[:, 2 * ROWS : 3 * ROWS] = to_tiles(factors[2], work)
    factor_out[:, 3 * ROWS : 4 * ROWS] = to_tiles(factors[3], work)
    ring_step(2, False)
    factor_in[me] = factor_out[me]
    plane_send(lambda peer: factor_out.at[peer], factor_in, 2)
    ring_step(3, False)
    relay(1)
    plane_send(lambda peer: small_out.at[peer], small_in, 3)
    ring_step(4, False)
    ring_step(5, False)
    relay(2)
    wait_many(factor_in, PLANE, 2)
    slab_factors[0] = gather_slab(factor_in[:, 0 * ROWS : 1 * ROWS]).astype(BF16)
    slab_factors[1] = gather_slab(factor_in[:, 1 * ROWS : 2 * ROWS]).astype(BF16)
    slab_factors[2] = gather_slab(factor_in[:, 2 * ROWS : 3 * ROWS]).astype(BF16)
    slab_factors[3] = gather_slab(factor_in[:, 3 * ROWS : 4 * ROWS]).astype(BF16)
    ring_step(6, False)
    relay(3)
    wait_many(small_in, PLANE, 3)
    small_half[...] = jnp.sum(small_in[...].astype(F32), axis=0).astype(BF16)
    small_ring[z] = small_half[...]
    ring_step(7, True)
    ring_share(small_half, small_ring, 4, False)
    relay(4)
    relay(5)
    for slot in range(SLOTS):
        await_hop(slot // 2, RING // 2, slot)
    ring_copy(small_half, small_ring, RING // 2, 4).start()
    contract([lax.rem(z + RING // 2, RING)])

    left_grad = left_sums[...].T
    for n in range(2):
        values = left_grad if n == 0 else right_sums[...]
        values = values.astype(BF16).astype(F32)
        for m in range(2):
            terms = values * slab_factors[2 * n + m].astype(F32)
            for g in range(4):
                slab_proj[g, (2 * n + m) * WIDTH : (2 * n + m + 1) * WIDTH] = terms[
                    :, g * 128 : (g + 1) * 128
                ]
    relay(6)
    total = jnp.zeros((4 * SLOTS, WIDTH), F32)
    for k in range(BANKS * ROWS):
        terms = jnp.concatenate(
            [slab_proj[g, pl.ds(k, 4 * SLOTS, stride=BANKS * ROWS), :] for g in range(4)], axis=1
        )
        pairs = pairs_all[k // ROWS, k % ROWS].reshape(TOKENS, WIDTH)
        total = total + mm(terms.astype(BF16), pairs, 1, 0)
    win_half[...] = total.astype(BF16)
    win_ring[z] = win_half[...]
    ring_share(win_half, win_ring, 5)

    back_out[:, :ROWS] = scatter_slab(left_grad)
    back_out[:, ROWS:] = scatter_slab(right_sums[...])
    back_in[me] = back_out[me]
    plane_send(lambda peer: back_out.at[peer], back_in, 6)

    def ring_total(ring):
        return jnp.sum(ring[...].astype(F32), axis=0) * (1.0 / TOKENS)

    wait_many(small_ring, RING, 4)
    small_mine[...] = ring_total(small_ring)
    dgain_ref[...] = small_mine[8:9]
    saves[3].start()
    small_all[me] = small_mine[:8]
    plane_send(lambda peer: small_mine.at[pl.ds(0, 8)], small_all, 7)

    settle()
    for way in range(2):
        wait_bytes(held.at[pl.ds(0, RING - 1), pl.ds(0, 2)], ring_send.at[way])
    wait_many(win_ring, RING, 5)
    win_mine[...] = ring_total(win_ring).astype(BF16)
    win_all[me] = win_mine[...]
    plane_send(lambda peer: win_mine, win_all, 8)

    wait_many(back_in, PLANE, 6)
    grad_left = from_tiles(back_in[:, :ROWS], work)
    proj[:WIDTH] = (grad_left * factors[0]).astype(BF16)
    proj[WIDTH : 2 * WIDTH] = (grad_left * factors[1]).astype(BF16)
    grad_right = from_tiles(back_in[:, ROWS:], work)
    proj[2 * WIDTH : 3 * WIDTH] = (grad_right * factors[2]).astype(BF16)
    proj[3 * WIDTH : 4 * WIDTH] = (grad_right * factors[3]).astype(BF16)
    weights = jnp.concatenate([win_ref[...], wgate_ref[...]], axis=1)
    d_pair = mm(weights, proj[...], 1, 0)
    dpair_ref[...] = d_pair.T.astype(BF16).reshape(ROWS, COLS, WIDTH)
    saves[0].start()

    wait_bytes(pairs_all.at[0, :, pl.ds(0, ACROSS - 1)], x_send.at[0])
    wait_bytes(pairs_all.at[0], x_send.at[1])
    wait_many(small_all, PLANE, 7)
    dsmall_ref[...] = small_all[...].reshape(2 * WIDTH, WIDTH)
    saves[2].start()
    wait_many(win_all, PLANE, 8)
    work[...] = win_all[...].astype(F32).reshape(4 * WIDTH, WIDTH)
    dwin_ref[...] = jnp.concatenate(
        [work[pl.ds(n, PLANE, stride=4 * SLOTS), :] for n in range(4 * SLOTS)], axis=0
    ).T
    saves[1].start()
    settle()
    for save in saves:
        save.wait()


def finish(dpair, dwin, dsmall, dgain, dpair_out, dwin_out, dwgate_out, dwout_out, dgain_out, *rest):
    held, loads, saves = rest[:4], rest[4], rest[5]
    sources = [dpair, dwin, dsmall, dgain]
    first = [
        pltpu.make_async_copy(source, target, loads.at[k])
        for k, (source, target) in enumerate(zip(sources, held))
    ]
    last = [
        pltpu.make_async_copy(source, target, saves.at[k])
        for k, (source, target) in enumerate(
            [
                (held[0], dpair_out),
                (held[1], dwin_out),
                (held[2].at[pl.ds(0, WIDTH)], dwgate_out),
                (held[2].at[pl.ds(WIDTH, WIDTH)], dwout_out),
                (held[3], dgain_out),
            ]
        )
    ]
    for copy in first:
        copy.start()
    for k, copies in enumerate([last[:1], last[1:2], last[2:4], last[4:]]):
        first[k].wait()
        for copy in copies:
            copy.start()
    for copy in last:
        copy.wait()


def shards(pair_norm, out_hat, out_rstd, grad_out, token_mask, w_in, w_gate, w_out, ln_gain):
    tile = (ROWS, COLS, WIDTH)
    square = (WIDTH, WIDTH)
    hbm = pl.BlockSpec(memory_space=pltpu.HBM)
    shape = jax.ShapeDtypeStruct
    tiles = lambda rows, dtype: pltpu.VMEM((PLANE, rows, WIDTH), dtype)
    results = pl.pallas_call(
        kernel,
        out_shape=(
            shape(tile, BF16),
            shape((WIDTH, 4 * WIDTH), F32),
            shape((2 * WIDTH, WIDTH), F32),
            shape((1, WIDTH), F32),
        ),
        in_specs=[hbm] * 9,
        out_specs=[hbm] * 4,
        scratch_shapes=[
            pltpu.VMEM(tile, BF16),
            pltpu.VMEM(tile, BF16),
            pltpu.VMEM((ROWS, COLS), F32),
            pltpu.VMEM(tile, BF16),
            pltpu.VMEM((1, TOKENS), jnp.int32),
            pltpu.VMEM((WIDTH, 4 * WIDTH), BF16),
            pltpu.VMEM(square, BF16),
            pltpu.VMEM(square, BF16),
            pltpu.VMEM((1, WIDTH), F32),
            pltpu.VMEM(tile, BF16),
            pltpu.VMEM((WIDTH, 4 * WIDTH), F32),
            pltpu.VMEM((2 * WIDTH, WIDTH), F32),
            pltpu.VMEM((1, WIDTH), F32),
            pltpu.VMEM((PAIRS, WIDTH), F32),
            *[tiles(ROWS, BF16)] * 2,
            *[tiles(2 * ROWS, BF16)] * 2,
            *[tiles(4 * ROWS, BF16)] * 2,
            *[tiles(2 * ROWS, BF16)] * 2,
            pltpu.VMEM((RING, SLOTS, BANKS * ROWS, TOKENS), BF16),
            pltpu.VMEM((WIDTH, SLOTS * TOKENS), BF16),
            pltpu.VMEM((TOKENS, WIDTH), BF16),
            pltpu.VMEM((TOKENS, WIDTH), F32),
            pltpu.VMEM((WIDTH, TOKENS), F32),
            pltpu.VMEM((4, WIDTH, PAIRS), F32),
            pltpu.VMEM((4, WIDTH, TOKENS), BF16),
            pltpu.VMEM((4, 4 * WIDTH, 128), F32),
            pltpu.VMEM((5 * WIDTH, PAIRS), BF16),
            pltpu.VMEM((BANKS, ROWS, ACROSS, COLS, WIDTH), BF16),
            tiles(ROWS, BF16),
            tiles(ROWS, BF16),
            pltpu.VMEM((ROWS, WIDTH), BF16),
            pltpu.VMEM((RING, ROWS, WIDTH), BF16),
            pltpu.VMEM((ROWS, WIDTH), F32),
            tiles(8, F32),
            pltpu.VMEM((ROWS, WIDTH), BF16),
            pltpu.VMEM((RING, ROWS, WIDTH), BF16),
            pltpu.VMEM((ROWS, WIDTH), BF16),
            tiles(ROWS, BF16),
            pltpu.SemaphoreType.DMA((9,)),
            pltpu.SemaphoreType.DMA((4,)),
            pltpu.SemaphoreType.DMA((2,)),
            pltpu.SemaphoreType.DMA((2, RING // 2, SLOTS)),
            pltpu.SemaphoreType.DMA((9,)),
            pltpu.SemaphoreType.DMA((9,)),
            pltpu.SemaphoreType.DMA((2,)),
            pltpu.SemaphoreType.DMA((56,)),
        ],
        compiler_params=pltpu.CompilerParams(
            collective_id=0, has_side_effects=True, vmem_limit_bytes=62 * 1024 * 1024
        ),
    )(
        pair_norm, out_hat, out_rstd, grad_out, token_mask.reshape(1, TOKENS),
        w_in, w_gate, w_out, ln_gain.reshape(1, WIDTH),
    )
    d_pair, d_win, d_wgate, d_wout, d_gain = pl.pallas_call(
        finish,
        out_shape=(
            shape(tile, BF16),
            shape((WIDTH, 4 * WIDTH), F32),
            shape(square, F32),
            shape(square, F32),
            shape((1, WIDTH), F32),
        ),
        in_specs=[hbm] * 4,
        out_specs=[hbm] * 5,
        scratch_shapes=[
            pltpu.VMEM(tile, BF16),
            pltpu.VMEM((WIDTH, 4 * WIDTH), F32),
            pltpu.VMEM((2 * WIDTH, WIDTH), F32),
            pltpu.VMEM((1, WIDTH), F32),
            pltpu.SemaphoreType.DMA((4,)),
            pltpu.SemaphoreType.DMA((5,)),
        ],
        compiler_params=pltpu.CompilerParams(vmem_limit_bytes=62 * 1024 * 1024),
    )(*results)
    return d_pair, d_win, d_wgate, d_wout, d_gain.reshape(WIDTH)


def solution(mesh):
    tile = P("row", "col", None)
    in_specs = (tile, tile, P("row", "col"), tile, P(), P(), P(), P(), P())
    out_specs = (tile, P(), P(), P(), P())
    return jax.shard_map(shards, mesh=mesh, in_specs=in_specs, out_specs=out_specs, check_vma=False)
```
